32 devices in a mesh: groups: 2 (over y), ctx: 4 (over z), head: 2 (over x), pair: 2 (over core).
Axes of the slice: x: 2, y: 2, z: 4, core: 2. Of those that a mesh axis runs over, the one named last changes fastest.
Arguments:
- queries: bfloat16 [4096, 16, 128], P(('groups', 'ctx', 'pair'), 'head'), parts along dimension 0, may hold values from -5 to 5
- key_vectors: bfloat16 [4096, 16, 128], P(('groups', 'ctx', 'pair'), 'head'), parts along dimension 0, may hold values from -5 to 5
- value_vectors: bfloat16 [4096, 16, 128], P(('groups', 'ctx', 'pair'), 'head'), parts along dimension 0, may hold values from -6 to 6
- targets: bfloat16 [4096, 16, 128], P(('groups', 'ctx', 'pair'), 'head'), parts along dimension 0, may hold values from -6 to 6
- token_weights: int32 [4096], P(('groups', 'ctx', 'pair')), parts along dimension 0, may hold values from 0 to 3
- sessions: int32 [4096], P(('groups', 'ctx', 'pair')), parts along dimension 0, may hold values from 0 to 5, never falling along the last dimension, each value on 1 to 682 neighbouring positions
- window_size: int32 [16], P('head'), may hold values from 256 to 1024, as said below
Outputs:
- attended: bfloat16 [4096, 16, 128], P(('groups', 'ctx', 'pair'), 'head'), parts along dimension 0
- grad_queries: bfloat16 [4096, 16, 128], P(('groups', 'ctx', 'pair'), 'head'), parts along dimension 0
- grad_keys: bfloat16 [4096, 16, 128], P(('groups', 'ctx', 'pair'), 'head'), parts along dimension 0
- grad_values: bfloat16 [4096, 16, 128], P(('groups', 'ctx', 'pair'), 'head'), parts along dimension 0
The draws below stay inside these ranges and needn't reach their ends.
There are 2 independent parts, one for each index of `groups`. The reference program is written for one: setup_inputs(seed, part) draws one part's arguments, and reference() takes and returns one part's arrays. A program takes and returns all parts, laid end to end along the dimension named above; an argument that names none is the same for every part. Nothing has to cross between parts.
Inputs may be any that keep to these rules, and one draw needn't show every extreme that they name: `window_size`: some head's window equals 1024.
All inputs are finite; a program needn't handle non-finite values.
Results may differ from the reference program's by a relative error of at most 0.02.
Values may be sent and summed in bfloat16 or wider, within the bound.
No kernel may reach another device: no remote copies, remote signals or barrier semaphores. Data moves between devices by JAX's collectives and lax.ppermute only.
A program may use at most 128 MiB of HBM per device.

```python
import math
import jax
import jax.numpy as jnp
import numpy as np
from jax import lax

HEADS = 16
HEAD_DIM = 128
L_DEV = 256
WIN = 1024
BLOCK = 128
SESSIONS = 6
SEQ = 2048


def draw_queries(key, part):
    key = jax.random.fold_in(key, 11)
    drawn = jnp.clip(jax.random.normal(key, (SEQ, HEADS, HEAD_DIM), jnp.float32), -4.5, 4.5)
    return drawn.astype(jnp.bfloat16)


def draw_key_vectors(key, part):
    key = jax.random.fold_in(key, 12)
    drawn = jnp.clip(jax.random.normal(key, (SEQ, HEADS, HEAD_DIM), jnp.float32), -4.5, 4.5)
    return drawn.astype(jnp.bfloat16)


def draw_window_size(key, part):
    key = jax.random.fold_in(key, 21)
    window_draw = jax.random.randint(jax.random.fold_in(key, 1), (HEADS,), WIN // 4, WIN + 1)
    widest = jax.random.randint(jax.random.fold_in(key, 2), (), 0, HEADS)
    return jnp.where(jnp.arange(HEADS) == widest, WIN, window_draw).astype(jnp.int32)


def set_ends(values, own_key, smallest, largest):
    longest = values.shape.index(max(values.shape))
    spots = []
    for shift in (0, 1):
        where = [jax.random.randint(jax.random.fold_in(own_key, axis), (), 0, length) for axis, length in enumerate(values.shape)]
        where[longest] = (where[longest] + shift) % values.shape[longest]
        spots.append(tuple(where))
    return values.at[spots[0]].set(smallest).at[spots[1]].set(largest)


def level_of(stream_key, shape, cuts, smallest, high):
    level = 1.0
    for dim, blocks in cuts:
        steps = jax.random.uniform(jax.random.fold_in(jax.random.fold_in(stream_key, 6), dim), (blocks,), jnp.float32, smallest / len(cuts), high / len(cuts))
        level = level * jnp.repeat(jnp.exp(steps), shape[dim] // blocks).reshape((-1,) + (1,) * (len(shape) - 1 - dim))
    return level


def length_profile(count, total, limit, skew):
    weights = [(1 << 20) // math.isqrt(grade ** skew) + 1 for grade in range(2, count + 1)]
    spare, holding = total - limit - (count - 1), [1] * (count - 1)
    while spare > 0:
        candidates = [i for i in range(count - 1) if holding[i] < limit]
        whole, left = sum([weights[i] for i in candidates]), spare
        for i in candidates:
            addition = min(limit - holding[i], max(1, left * weights[i] // whole), spare)
            holding[i] = holding[i] + addition
            spare = spare - addition
    return np.array([limit] + holding)


def ragged_sizes(own_key, number_of, total, reach, skew):
    if number_of == 2:
        one = jax.random.randint(own_key, (), max(1, total - reach), min(reach, total - 1) + 1)
        return jnp.stack([one, total - one])
    sizes = jnp.asarray(length_profile(number_of, total, reach, skew), jnp.int32)
    twos = (number_of - 1) // 2
    source_of, receiver = sizes[1:1 + 2 * twos:2], sizes[2:2 + 2 * twos:2]
    slack = jnp.minimum(source_of - 1, reach - receiver)
    shifted = jax.random.randint(jax.random.fold_in(own_key, 1), (twos,), 0, 1 << 20) % (slack + 1)
    sizes = sizes.at[1:1 + 2 * twos:2].set(source_of - shifted).at[2:2 + 2 * twos:2].set(receiver + shifted)
    return sizes[jax.random.permutation(jax.random.fold_in(own_key, 2), number_of)]


def gaussian(own_key, shape, spread, most, split=(), kind=jnp.bfloat16):
    values = spread * jax.random.normal(own_key, shape, jnp.float32)
    if split:
        values = values * level_of(own_key, shape, split, -0.22, 0.18)
    return jnp.clip(values, -most, most).astype(kind)


def setup_inputs(seed: int = 0, part: int = 0) -> dict:
    splits = jax.random.split(jax.random.key(seed), 8)
    own_keys = jax.random.split(jax.random.fold_in(splits[7], part), 8)
    return {
        "queries": draw_queries(jax.random.fold_in(jax.random.fold_in(splits[7], part), 71), part),
        "key_vectors": draw_key_vectors(jax.random.fold_in(jax.random.fold_in(splits[7], part), 71), part),
        "value_vectors": gaussian(own_keys[2], (SEQ, HEADS, HEAD_DIM), 1.0, 6.0, ((0, 8), (1, 2))),
        "targets": gaussian(own_keys[3], (SEQ, HEADS, HEAD_DIM), 1.0, 6.0, ((0, 8), (1, 2))),
        "token_weights": set_ends(jax.random.randint(own_keys[4], (SEQ,), 0, 4), jax.random.fold_in(own_keys[4], 1), 0, 3).astype(jnp.int32),
        "sessions": jnp.searchsorted(jnp.cumsum(ragged_sizes(own_keys[5], SESSIONS, SEQ, SEQ // 3, 2)), jnp.arange(SEQ), side="right").astype(jnp.int32),
        "window_size": draw_window_size(jax.random.fold_in(splits[7], 71), part),
    }


MASKED = -1e+30
EPSILON = 1e-06

def contract(form, left, right):
    return jnp.einsum(form, left.astype(jnp.float32), right.astype(jnp.float32))

def feature(values_in):
    raised = values_in.astype(jnp.float32)
    return jnp.where(raised > 0, raised + 1.0, jnp.exp(jnp.minimum(raised, 0.0)))

def feature_slope(values_in):
    raised = values_in.astype(jnp.float32)
    return jnp.where(raised > 0, 1.0, jnp.exp(jnp.minimum(raised, 0.0)))

def combine_states(early, late):
    session_a, summed_a = early
    session_b, summed_b = late
    keeping = jnp.logical_or(session_b < 0, session_a == session_b)
    factor = jnp.where(keeping, 1.0, 0.0).astype(summed_b.dtype)
    factor = factor.reshape(factor.shape + (1,) * (summed_b.ndim - factor.ndim))
    return (jnp.where(session_b < 0, session_a, session_b), summed_b + factor * summed_a)

def advance(running, incoming):
    return (combine_states(running, incoming), running)

def normalize(numerator):
    inverse_rms = lax.rsqrt(lax.optimization_barrier(jnp.mean(numerator * numerator, axis=-1, keepdims=True)) + EPSILON)
    return (numerator * inverse_rms, inverse_rms)

def linear_local(phi_q, phi_k, value_rows, sessions, block):
    length, head_count, head_width = phi_q.shape
    block_count = length // block
    phi_query = phi_q.reshape(block_count, block, head_count, head_width)
    phi_key = phi_k.reshape(block_count, block, head_count, head_width)
    value_blocks = value_rows.reshape(block_count, block, head_count, head_width)
    session_blocks = sessions.reshape(block_count, block)
    lower_tri = jnp.arange(block)[:, None] >= jnp.arange(block)[None, :]
    same_block = jnp.logical_and(lower_tri[None], session_blocks[:, :, None] == session_blocks[:, None, :])[:, None]
    alike_scores = jnp.where(same_block, contract('nchk,nshk->nhcs', phi_query, phi_key), 0.0).astype(jnp.bfloat16)
    within = contract('nhcs,nshd->nchd', alike_scores, value_blocks)
    last_session = session_blocks[:, -1]
    owned_rows = (session_blocks == last_session[:, None])[:, :, None, None]
    local_sum = contract('nchk,nchd->nhkd', jnp.where(owned_rows, phi_key, jnp.zeros_like(phi_key)), value_blocks)
    identity = (jnp.array(-1, jnp.int32), jnp.zeros(local_sum.shape[1:], jnp.float32))
    summary, starts = lax.scan(advance, identity, (last_session, local_sum))
    cache = (phi_query, phi_key, value_blocks, session_blocks, same_block, alike_scores, within, starts)
    return (cache, summary)

def linear_finish(cache, prefix):
    phi_query, phi_key, value_blocks, session_blocks, same_block, alike_scores, within, starts = cache
    start_session, start_state = combine_states(prefix, starts)
    rounded_start = start_state.astype(jnp.bfloat16)
    in_state = (session_blocks == start_session[:, None])[:, :, None, None]
    numerator = within + jnp.where(in_state, contract('nchk,nhkd->nchd', phi_query, rounded_start), 0.0)
    flat_shape = (-1,) + numerator.shape[2:]
    return (numerator.reshape(flat_shape), (start_session, rounded_start))

def linear_back_local(cache, grad_num):
    phi_query = cache[0]
    session_blocks = cache[3]
    grad_blocks = grad_num.reshape(phi_query.shape)
    first_session = session_blocks[:, 0]
    owned_rows = (session_blocks == first_session[:, None])[:, :, None, None]
    local_sum = contract('nchk,nchd->nhkd', jnp.where(owned_rows, phi_query, jnp.zeros_like(phi_query)), grad_blocks)
    identity = (jnp.array(-1, jnp.int32), jnp.zeros(local_sum.shape[1:], jnp.float32))
    summary, block_ends = lax.scan(advance, identity, (first_session, local_sum), reverse=True)
    return ((grad_blocks, block_ends), summary)

def linear_back_finish(cache, forward_state, returned, suffix):
    phi_query, phi_key, value_blocks, session_blocks, same_block, alike_scores = (cache[0], cache[1], cache[2], cache[3], cache[4], cache[5])
    start_session, rounded_start = forward_state
    grad_blocks, block_ends = returned
    end_session, end_state = combine_states(suffix, block_ends)
    later_state = end_state.astype(jnp.bfloat16)
    in_state = (session_blocks == start_session[:, None])[:, :, None, None]
    later_use = (session_blocks == end_session[:, None])[:, :, None, None]
    back_scores = jnp.where(same_block, contract('nchd,nshd->nhcs', grad_blocks, value_blocks), 0.0).astype(jnp.bfloat16)
    grad_phi_q = contract('nhcs,nshk->nchk', back_scores, phi_key) + jnp.where(in_state, contract('nchd,nhkd->nchk', grad_blocks, rounded_start), 0.0)
    grad_phi_k = contract('nhcs,nchk->nshk', back_scores, phi_query) + jnp.where(later_use, contract('nshd,nhkd->nshk', value_blocks, later_state), 0.0)
    grad_v_lin = contract('nhcs,nchd->nshd', alike_scores, grad_blocks) + jnp.where(later_use, contract('nshk,nhkd->nshd', phi_key, later_state), 0.0)
    flat_shape = (-1,) + grad_phi_q.shape[2:]
    return (grad_phi_q.reshape(flat_shape), grad_phi_k.reshape(flat_shape), grad_v_lin.reshape(flat_shape))

def window_head(query_rows, key_rows, value_rows, grad_rows, sessions, window_cap, block, reach_blocks):
    total_len, head_width = query_rows.shape
    block_count = total_len // block
    margin = reach_blocks * block
    span_len = margin + block
    factor = 1.0 / math.sqrt(head_width)
    padded_k = jnp.concatenate([jnp.zeros((margin, head_width), key_rows.dtype), key_rows])
    padded_v = jnp.concatenate([jnp.zeros((margin, head_width), value_rows.dtype), value_rows])
    padded_s = jnp.concatenate([jnp.zeros((margin,), jnp.int32), sessions])

    def visit(running, block_index):
        acc_k, acc_v = running
        start = (block_index * block).astype(jnp.int32)
        query_part = lax.dynamic_slice_in_dim(query_rows, start, block)
        grad_part = lax.dynamic_slice_in_dim(grad_rows, start, block)
        session_q = lax.dynamic_slice_in_dim(sessions, start, block)
        key_part = lax.dynamic_slice_in_dim(padded_k, start, span_len)
        value_part = lax.dynamic_slice_in_dim(padded_v, start, span_len)
        session_k = lax.dynamic_slice_in_dim(padded_s, start, span_len)
        query_pos = start + jnp.arange(block, dtype=jnp.int32)
        key_pos = start - margin + jnp.arange(span_len, dtype=jnp.int32)
        distance = query_pos[:, None] - key_pos[None, :]
        allowed = (key_pos[None, :] >= 0) & (distance >= 0) & (distance < window_cap) & (session_q[:, None] == session_k[None, :])
        scores = jnp.where(allowed, jnp.dot(query_part, key_part.T, preferred_element_type=jnp.float32) * factor, MASKED)
        new_peak = lax.optimization_barrier(jnp.max(scores, axis=-1, keepdims=True))
        exponent = jnp.exp(scores - new_peak)
        attn_prob = exponent / lax.optimization_barrier(jnp.sum(exponent, axis=-1, keepdims=True))
        rounded = attn_prob.astype(jnp.bfloat16)
        window_out = jnp.dot(rounded, value_part, preferred_element_type=jnp.float32)
        rowdot = lax.optimization_barrier(jnp.sum(grad_part.astype(jnp.float32) * window_out, axis=-1, keepdims=True))
        grad_prob = jnp.dot(grad_part, value_part.T, preferred_element_type=jnp.float32)
        dscore = (attn_prob * (grad_prob - rowdot)).astype(jnp.bfloat16)
        grad_q_win = jnp.dot(dscore, key_part, preferred_element_type=jnp.float32) * factor
        piece_key = lax.optimization_barrier((jnp.dot(dscore.T, query_part, preferred_element_type=jnp.float32) * factor).astype(jnp.bfloat16)).astype(jnp.float32)
        piece_value = lax.optimization_barrier(jnp.dot(rounded.T, grad_part, preferred_element_type=jnp.float32).astype(jnp.bfloat16)).astype(jnp.float32)
        acc_k = lax.dynamic_update_slice_in_dim(acc_k, lax.dynamic_slice_in_dim(acc_k, start, span_len) + piece_key, start, 0)
        acc_v = lax.dynamic_update_slice_in_dim(acc_v, lax.dynamic_slice_in_dim(acc_v, start, span_len) + piece_value, start, 0)
        return ((acc_k, acc_v), (window_out, grad_q_win))
    empty = jnp.zeros((margin + total_len, head_width), jnp.float32)
    sums, outputs = lax.scan(visit, (empty, empty), jnp.arange(block_count))
    return (outputs[0].reshape(total_len, head_width), outputs[1].reshape(total_len, head_width), sums[0][margin:], sums[1][margin:])

def reference(queries, key_vectors, value_vectors, targets, token_weights, sessions, window_size):
    grad_out = (token_weights[:, None, None].astype(jnp.float32) * targets.astype(jnp.float32)).astype(jnp.bfloat16)

    def per_head(per_items):
        query_rows, key_rows, value_rows, grad_rows, window_cap = per_items
        phi_q = feature(query_rows).astype(jnp.bfloat16)[:, None]
        phi_k = feature(key_rows).astype(jnp.bfloat16)[:, None]
        cache, summary = linear_local(phi_q, phi_k, value_rows[:, None], sessions, BLOCK)
        identity = (jnp.array(-1, jnp.int32), jnp.zeros_like(summary[1]))
        numerator, forward_state = linear_finish(cache, identity)
        linear_out, inverse_rms = normalize(numerator)
        window_out, grad_q_win, grad_k_win, grad_v_win = window_head(query_rows, key_rows, value_rows, grad_rows, sessions, window_cap, L_DEV, WIN // L_DEV)
        grad_full = grad_rows.astype(jnp.float32)[:, None]
        grad_num = inverse_rms * (grad_full - linear_out * lax.optimization_barrier(jnp.mean(grad_full * linear_out, axis=-1, keepdims=True)))
        returned, summary_back = linear_back_local(cache, grad_num.astype(jnp.bfloat16))
        grad_phi_q, grad_phi_k, grad_v_lin = linear_back_finish(cache, forward_state, returned, identity)
        combined = (linear_out[:, 0] + window_out).astype(jnp.bfloat16)
        grad_query = (feature_slope(query_rows) * grad_phi_q[:, 0] + grad_q_win).astype(jnp.bfloat16)
        grad_key = (feature_slope(key_rows) * grad_phi_k[:, 0] + grad_k_win).astype(jnp.bfloat16)
        grad_value = (grad_v_lin[:, 0] + grad_v_win).astype(jnp.bfloat16)
        return (combined, grad_query, grad_key, grad_value)
    results = lax.map(per_head, (jnp.swapaxes(queries, 0, 1), jnp.swapaxes(key_vectors, 0, 1), jnp.swapaxes(value_vectors, 0, 1), jnp.swapaxes(grad_out, 0, 1), window_size))
    return (jnp.swapaxes(results[0], 0, 1), jnp.swapaxes(results[1], 0, 1), jnp.swapaxes(results[2], 0, 1), jnp.swapaxes(results[3], 0, 1))
```

```python
import functools
import math

import jax
import jax.numpy as jnp
from jax import lax
from jax.experimental import pallas as pl
from jax.experimental.pallas import tpu as pltpu
from jax.sharding import PartitionSpec as P

WIN = 1024
SESSIONS = 6
EPSILON = 1e-06
MASKED = -1e30
AXES = ("ctx", "pair")
EXTRA = 16
LANES = 128

f32 = jnp.float32
bf16 = jnp.bfloat16


def dot(a, b):
    return lax.dot_general(a, b, (((1,), (0,)), ((), ())), preferred_element_type=f32)


def dot_t(a, b):
    return lax.dot_general(a, b, (((1,), (1,)), ((), ())), preferred_element_type=f32)


def t_dot(a, b):
    return lax.dot_general(a, b, (((0,), (0,)), ((), ())), preferred_element_type=f32)


def feature(x):
    return jnp.where(x > 0, x + 1.0, jnp.exp(jnp.minimum(x, 0.0)))


def slope(x):
    return jnp.where(x > 0, 1.0, jnp.exp(jnp.minimum(x, 0.0)))


def row_of(column):
    n = column.shape[0]
    return jnp.concatenate(
        [
            jnp.transpose(jnp.broadcast_to(column[i : i + LANES], (LANES, LANES)))[0:1]
            for i in range(0, n, LANES)
        ],
        axis=1,
    )


def column_of(rows):
    return jnp.concatenate(
        [
            jnp.transpose(jnp.broadcast_to(rows[i : i + 1], (LANES, LANES)))[:, 0:1]
            for i in range(rows.shape[0])
        ],
        axis=0,
    )


class Plan:
    def __init__(self, length, heads, width, total):
        self.length = length
        self.heads = heads
        self.half = heads // 2
        self.width = width
        self.chip = 2 * length
        longest = total // 3
        reach = min(WIN, longest) - 1
        tail = max(reach - self.chip, 0)
        self.far = longest - 1 > 2 * self.chip or longest - 1 > reach
        self.merged = tail <= length
        self.tail = -(-tail // 16) * 16 if self.merged else length
        self.tail_fill = length if self.merged else self.chip
        self.before = self.tail_fill + self.chip
        self.code_rows = length // LANES
        self.stat_rows = -(-(2 * self.half * self.chip // LANES) // 16) * 16
        self.state_rows = self.half * width
        self.rows = self.half * 2 * length + EXTRA
        self.tail_rows = self.half * 2 * self.tail + EXTRA


def pack_body(p, core_ref, q_ref, k_ref, v_ref, t_ref, w_ref, s_ref, *rest):
    kv_same, kv_cross, qg_same, qg_cross = rest[:4]
    scratch = rest[-1]
    core = core_ref[0]
    L = p.length
    weight = column_of(w_ref[...].astype(f32))
    for n, ref in enumerate((k_ref, v_ref, q_ref, t_ref)):
        x = jnp.swapaxes(ref[...].astype(f32), 0, 1)
        if n == 3:
            x = x * weight[None]
        scratch[n] = x.astype(bf16)
    codes = jnp.concatenate(
        [s_ref[...].astype(f32) + 1.0, jnp.zeros((EXTRA - p.code_rows, LANES), f32)], axis=0
    ).astype(bf16)
    for out, first, which in (
        (kv_same, 0, core),
        (kv_cross, 0, 1 - core),
        (qg_same, 2, core),
        (qg_cross, 2, 1 - core),
    ):
        for h in range(p.half):
            for n in range(2):
                at = (2 * h + n) * L
                out[at : at + L, :] = scratch[first + n, which * p.half + h]
        out[p.rows - EXTRA :, :] = codes
    if p.merged:
        for out, which in ((rest[4], core), (rest[5], 1 - core)):
            for first, wanted, lead in ((0, 1, L - p.tail), (2, 0, 0)):

                @pl.when(core == wanted)
                def _():
                    for h in range(p.half):
                        for n in range(2):
                            at = (2 * h + n) * p.tail
                            out[at : at + p.tail, :] = scratch[
                                first + n, which * p.half + h, lead : lead + p.tail
                            ]

            out[p.tail_rows - EXTRA :, :] = codes


def pack(p, core, q, k, v, targets, weights, sessions):
    big = jax.ShapeDtypeStruct((p.rows, p.width), bf16)
    outs = [big] * 4
    if p.merged:
        outs += [jax.ShapeDtypeStruct((p.tail_rows, p.width), bf16)] * 2
    vmem = pl.BlockSpec(memory_space=pltpu.VMEM)
    return pl.pallas_call(
        functools.partial(pack_body, p),
        out_shape=outs,
        in_specs=[pl.BlockSpec(memory_space=pltpu.SMEM)] + [vmem] * 6,
        out_specs=[vmem] * len(outs),
        scratch_shapes=[pltpu.VMEM((4, p.heads, p.length, p.width), bf16)],
        compiler_params=pltpu.CompilerParams(vmem_limit_bytes=40 << 20),
        name="pack",
    )(core, q, k, v, targets, weights, sessions)


def code_block(p, ref, rows):
    return ref[rows - EXTRA :, :].astype(f32)[: p.code_rows]


def flat(rows):
    return jnp.concatenate([rows[i : i + 1] for i in range(rows.shape[0])], axis=1)


def in_order(core, same, cross):
    first = jnp.where(core == 0, same, cross)
    second = jnp.where(core == 0, cross, same)
    return jnp.concatenate([first, second], axis=0)


def place(p, core, head, same, cross, dst_a, dst_b, start):
    L = p.length
    for ref, which in ((same, core), (cross, 1 - core)):
        to = pl.ds(pl.multiple_of(start + which * L, 16), L)
        for n, dst in ((0, dst_a), (1, dst_b)):
            dst[to, :] = ref[pl.ds(pl.multiple_of((2 * head + n) * L, 16), L), :]


def place_tail(p, flag, head, one, two, dst_a, dst_b, start):
    for n, dst in ((0, dst_a), (1, dst_b)):
        rows = pl.ds(pl.multiple_of((2 * head + n) * p.tail, 16), p.tail)
        dst[start : start + p.tail, :] = jnp.where(flag, one[rows, :], two[rows, :])


def forward_body(p, core_ref, win_ref, *refs):
    kv_own, qg_own, kv_pair, qg_pair, kv_n_same, kv_n_cross, t_a, t_b = refs[:8]
    refs = refs[8:]
    if p.far:
        far_ref, refs = refs[0], refs[1:]
    att_keep, att_send, gn_out, message, ks, vs, qs, gs, atts, dqs, stat, lo_s, code_s = refs
    core = core_ref[0]
    L, C, B, D = p.length, p.chip, p.before, p.width
    scale = 1.0 / math.sqrt(D)
    c2 = scale * math.log2(math.e)

    own_codes = in_order(core, code_block(p, kv_own, p.rows), code_block(p, kv_pair, p.rows))
    near_codes = in_order(
        core, code_block(p, kv_n_same, p.rows), code_block(p, kv_n_cross, p.rows)
    )
    if p.merged:
        far_codes = jnp.where(
            core == 0, code_block(p, t_a, p.tail_rows), code_block(p, t_b, p.tail_rows)
        )
    else:
        far_codes = in_order(core, code_block(p, t_a, p.rows), code_block(p, t_b, p.rows))
    halo_codes = flat(jnp.concatenate([far_codes, near_codes], axis=0))
    own_row = flat(own_codes)
    code = column_of(own_codes)
    last = halo_codes[:, B - 1 : B]
    first_own = own_row[:, 0:1]
    valid = jnp.sum(jnp.where(halo_codes > 0, 1.0, 0.0), axis=1, keepdims=True)
    before_count = jnp.sum(
        jnp.where(jnp.logical_and(halo_codes > 0, halo_codes < code), 1.0, 0.0),
        axis=1,
        keepdims=True,
    ) + jnp.sum(jnp.where(own_row < code, 1.0, 0.0), axis=1, keepdims=True)
    lo_s[...] = (before_count - valid).astype(jnp.int32)
    code_s[...] = code
    cont = jnp.sum(
        jnp.where(jnp.logical_and(halo_codes == last, halo_codes > 0), 1.0, 0.0),
        axis=1,
        keepdims=True,
    ).astype(jnp.int32)
    halo_pos = lax.broadcasted_iota(jnp.int32, (B, 1), 0) - B
    in_start = jnp.broadcast_to(halo_pos >= -cont, (B, D))
    if p.merged and p.tail < p.tail_fill:
        gap = p.tail_fill - p.tail
        ks[0:gap, :] = jnp.zeros((gap, D), bf16)
        vs[0:gap, :] = jnp.zeros((gap, D), bf16)

    @pl.loop(0, p.half)
    def _(h):
        place(p, core, h, kv_own, kv_pair, ks, vs, B)
        place(p, core, h, kv_n_same, kv_n_cross, ks, vs, p.tail_fill)
        place(p, core, h, qg_own, qg_pair, qs, gs, 0)
        if p.merged:
            place_tail(p, core == 0, h, t_a, t_b, ks, vs, p.tail_fill - p.tail)
        else:
            place(p, core, h, t_a, t_b, ks, vs, 0)
        window = win_ref[h]
        if p.far:
            start_state = far_ref[pl.ds(pl.multiple_of(h * D, 16), D), :]
        else:
            halo_phi = jnp.where(in_start, feature(ks[0:B, :].astype(f32)), 0.0).astype(bf16)
            start_state = t_dot(halo_phi, vs[0:B, :]).astype(bf16)
        phi_k = feature(ks[B:, :].astype(f32)).astype(bf16)
        state = jnp.zeros((D, D), f32)
        for r in range(2):
            rows = slice(r * L, (r + 1) * L)
            q = qs[rows, :]
            g = gs[rows, :]
            gf = g.astype(f32)
            lo = lo_s[rows, :]
            mine = code_s[rows, :]
            t_pos = lax.broadcasted_iota(jnp.int32, (L, 1), 0) + r * L
            begin = 0 if not p.merged else r * L
            n_halo = B - begin
            n_own = (r + 1) * L
            wide = n_halo + n_own
            k_part = ks[begin : begin + wide, :]
            v_part = vs[begin : begin + wide, :]
            s_pos = lax.broadcasted_iota(jnp.int32, (L, wide), 1) + (begin - B)
            low = jnp.maximum(lo, t_pos - window + 1)
            allowed = jnp.logical_and(s_pos >= low, s_pos <= t_pos)
            score = jnp.where(allowed, dot_t(q, k_part), MASKED)
            peak = jnp.max(score, axis=1, keepdims=True)
            e = jnp.exp2(score * c2 - peak * c2)
            total = jnp.sum(e, axis=1, keepdims=True)
            inverse = 1.0 / total
            window_out = dot(e.astype(bf16), v_part) * inverse
            rowdot = jnp.sum(gf * window_out, axis=1, keepdims=True)
            ds = (e * (dot_t(g, v_part) - rowdot)).astype(bf16)
            dq = dot(ds, k_part) * (inverse * scale)
            lse = peak * c2 + jnp.log2(total)
            for which, column in ((0, lse), (1, rowdot)):
                base = (which * p.half + h) * (C // LANES) + r * (L // LANES)
                row = row_of(column)
                for j in range(L // LANES):
                    stat[pl.ds(base + j, 1), :] = row[:, j * LANES : (j + 1) * LANES]
            qf = q.astype(f32)
            phi_q = feature(qf).astype(bf16)
            own_pos = lax.broadcasted_iota(jnp.int32, (L, n_own), 1)
            alike = jnp.logical_and(own_pos >= lo, own_pos <= t_pos)
            a = jnp.where(alike, dot_t(phi_q, phi_k[:n_own]), 0.0).astype(bf16)
            reads = mine == last
            numerator = dot(a, vs[B : B + n_own, :]) + jnp.where(
                reads, dot(phi_q, start_state), 0.0
            )
            inverse_rms = lax.rsqrt(
                jnp.mean(numerator * numerator, axis=1, keepdims=True) + EPSILON
            )
            linear_out = numerator * inverse_rms
            grad_num = (
                inverse_rms
                * (gf - linear_out * jnp.mean(gf * linear_out, axis=1, keepdims=True))
            ).astype(bf16)
            b = jnp.where(alike, dot_t(grad_num, vs[B : B + n_own, :]), 0.0).astype(bf16)
            grad_phi_q = dot(b, phi_k[:n_own]) + jnp.where(
                reads, dot_t(grad_num, start_state), 0.0
            )
            atts[h, rows, :] = (linear_out + window_out).astype(bf16)
            dqs[h, rows, :] = (slope(qf) * grad_phi_q + dq).astype(bf16)
            gn_out[h, rows, :] = grad_num
            opening = mine == first_own
            state = state + t_dot(jnp.where(opening, phi_q, jnp.zeros_like(phi_q)), grad_num)
        message[pl.ds(pl.multiple_of(h * D, 16), D), :] = state.astype(bf16)

    values = stat[...]
    if 2 * p.half * C // LANES < p.stat_rows:
        used = lax.broadcasted_iota(jnp.int32, values.shape, 0) < 2 * p.half * C // LANES
        values = jnp.where(used, values, 0.0)
    for n in range(3):
        piece = values.astype(bf16)
        at = p.state_rows + n * p.stat_rows
        message[at : at + p.stat_rows, :] = piece
        values = values - piece.astype(f32)
    for h in range(p.half):
        for n, src in ((0, atts), (1, dqs)):
            att_keep[n, h] = src[h, pl.ds(pl.multiple_of(core * L, 16), L), :]
            att_send[n, h] = src[h, pl.ds(pl.multiple_of((1 - core) * L, 16), L), :]


def forward(p, core, windows, payloads, far_state):
    vmem = pl.BlockSpec(memory_space=pltpu.VMEM)
    smem = pl.BlockSpec(memory_space=pltpu.SMEM)
    half = jax.ShapeDtypeStruct((2, p.half, p.length, p.width), bf16)
    outs = [
        half,
        half,
        jax.ShapeDtypeStruct((p.half, p.chip, p.width), bf16),
        jax.ShapeDtypeStruct((p.state_rows + 3 * p.stat_rows, p.width), bf16),
    ]
    extra = [far_state] if p.far else []
    span = p.before + p.chip
    return pl.pallas_call(
        functools.partial(forward_body, p),
        out_shape=outs,
        in_specs=[smem, smem] + [vmem] * (8 + len(extra)),
        out_specs=[vmem] * 4,
        scratch_shapes=[
            pltpu.VMEM((span, p.width), bf16),
            pltpu.VMEM((span, p.width), bf16),
            pltpu.VMEM((p.chip, p.width), bf16),
            pltpu.VMEM((p.chip, p.width), bf16),
            pltpu.VMEM((p.half, p.chip, p.width), bf16),
            pltpu.VMEM((p.half, p.chip, p.width), bf16),
            pltpu.VMEM((p.stat_rows, p.width), f32),
            pltpu.VMEM((p.chip, 1), jnp.int32),
            pltpu.VMEM((p.chip, 1), f32),
        ],
        compiler_params=pltpu.CompilerParams(vmem_limit_bytes=40 << 20),
        name="forward",
    )(core, windows, *payloads, *extra)


def stats_of(p, ref, head, count):
    result = []
    for which in range(2):
        base = (which * p.half + head) * (p.chip // LANES)
        result.append(flat(ref[pl.ds(base, p.chip // LANES), :])[:, :count])
    return result


def unpack_stats(p, message, dst):
    total = jnp.zeros((p.stat_rows, LANES), f32)
    for n in reversed(range(3)):
        at = p.state_rows + n * p.stat_rows
        total = total + message[at : at + p.stat_rows, :].astype(f32)
    dst[...] = total


def key_side(k, v, q, g, lse, rowdot, allowed, c2, scale):
    score = jnp.where(allowed, dot_t(k, q), MASKED)
    prob = jnp.exp2(score * c2 - lse)
    ds = (prob * (dot_t(v, g) - rowdot)).astype(bf16)
    return dot(ds, q) * scale, dot(prob.astype(bf16), g)


def own_body(p, core_ref, win_ref, kv_own, qg_own, kv_pair, qg_pair, gn, message, dk_o, dv_o, *s):
    ks, vs, qs, gs, stat, hi_s = s
    core = core_ref[0]
    L, C, D = p.length, p.chip, p.width
    scale = 1.0 / math.sqrt(D)
    c2 = scale * math.log2(math.e)
    own_codes = in_order(core, code_block(p, kv_own, p.rows), code_block(p, kv_pair, p.rows))
    own_row = flat(own_codes)
    code = column_of(own_codes)
    hi_s[...] = (
        jnp.sum(jnp.where(own_row <= code, 1.0, 0.0), axis=1, keepdims=True).astype(jnp.int32) - 1
    )
    unpack_stats(p, message, stat)

    @pl.loop(0, p.half)
    def _(h):
        place(p, core, h, kv_own, kv_pair, ks, vs, 0)
        place(p, core, h, qg_own, qg_pair, qs, gs, 0)
        window = win_ref[h]
        lse, rowdot = stats_of(p, stat, h, C)
        phi_q = feature(qs[...].astype(f32)).astype(bf16)
        for r in range(2):
            rows = slice(r * L, (r + 1) * L)
            after = slice(r * L, C)
            wide = C - r * L
            k, v = ks[rows, :], vs[rows, :]
            q, g = qs[after, :], gs[after, :]
            grad_num = gn[h, after, :]
            hi = hi_s[rows, :]
            s_pos = lax.broadcasted_iota(jnp.int32, (L, 1), 0) + r * L
            t_pos = lax.broadcasted_iota(jnp.int32, (L, wide), 1) + r * L
            alike = jnp.logical_and(t_pos >= s_pos, t_pos <= hi)
            allowed = jnp.logical_and(alike, t_pos < s_pos + window)
            dk, dv = key_side(
                k, v, q, g, lse[:, after], rowdot[:, after], allowed, c2, scale
            )
            kf = k.astype(f32)
            a = jnp.where(alike, dot_t(feature(kf).astype(bf16), phi_q[after]), 0.0).astype(bf16)
            b = jnp.where(alike, dot_t(v, grad_num), 0.0).astype(bf16)
            dk_o[h, rows, :] = dk + slope(kf) * dot(b, phi_q[after])
            dv_o[h, rows, :] = dv + dot(a, grad_num)


def own_keys(p, core, windows, kv_own, qg_own, kv_pair, qg_pair, gn, message):
    vmem = pl.BlockSpec(memory_space=pltpu.VMEM)
    smem = pl.BlockSpec(memory_space=pltpu.SMEM)
    full = jax.ShapeDtypeStruct((p.half, p.chip, p.width), f32)
    tile = pltpu.VMEM((p.chip, p.width), bf16)
    return pl.pallas_call(
        functools.partial(own_body, p),
        out_shape=[full, full],
        in_specs=[smem, smem] + [vmem] * 6,
        out_specs=[vmem] * 2,
        scratch_shapes=[tile] * 4
        + [pltpu.VMEM((p.stat_rows, p.width), f32), pltpu.VMEM((p.chip, 1), jnp.int32)],
        compiler_params=pltpu.CompilerParams(vmem_limit_bytes=40 << 20),
        name="own_keys",
    )(core, windows, kv_own, qg_own, kv_pair, qg_pair, gn, message)


def later_body(p, core_ref, win_ref, *refs):
    kv_own, kv_pair, qg_n_same, qg_n_cross, t_a, t_b, message_1, message_2, dk_i, dv_i = refs[:10]
    refs = refs[10:]
    if p.far:
        far_ref, refs = refs[0], refs[1:]
    keep, send, ks, vs, qs, gs, stat_1, stat_2, hi_s, code_s, dks, dvs = refs
    core = core_ref[0]
    L, C, D = p.length, p.chip, p.width
    N = p.tail_fill
    scale = 1.0 / math.sqrt(D)
    c2 = scale * math.log2(math.e)
    own_codes = in_order(core, code_block(p, kv_own, p.rows), code_block(p, kv_pair, p.rows))
    near_codes = in_order(
        core, code_block(p, qg_n_same, p.rows), code_block(p, qg_n_cross, p.rows)
    )
    if p.merged:
        far_codes = jnp.where(
            core == 1, code_block(p, t_a, p.tail_rows), code_block(p, t_b, p.tail_rows)
        )
    else:
        far_codes = in_order(core, code_block(p, t_a, p.rows), code_block(p, t_b, p.rows))
    after_row = flat(jnp.concatenate([near_codes, far_codes], axis=0))
    own_row = flat(own_codes)
    code = column_of(own_codes)
    code_s[...] = code
    hi_s[...] = (
        C
        - 1
        + jnp.sum(
            jnp.where(jnp.logical_and(after_row > 0, after_row <= code), 1.0, 0.0),
            axis=1,
            keepdims=True,
        )
        - jnp.sum(jnp.where(own_row > code, 1.0, 0.0), axis=1, keepdims=True) * (2.0 * (C + N))
    ).astype(jnp.int32)
    first_next = after_row[:, 0:1]
    goes_on = jnp.logical_and(first_next > 0, first_next == after_row[:, C : C + 1])
    unpack_stats(p, message_1, stat_1)
    unpack_stats(p, message_2, stat_2)
    if p.merged and p.tail < p.tail_fill:
        gap = p.tail_fill - p.tail
        qs[C + p.tail :, :] = jnp.zeros((gap, D), bf16)
        gs[C + p.tail :, :] = jnp.zeros((gap, D), bf16)

    @pl.loop(0, p.half)
    def _(h):
        place(p, core, h, kv_own, kv_pair, ks, vs, 0)
        place(p, core, h, qg_n_same, qg_n_cross, qs, gs, 0)
        if p.merged:
            place_tail(p, core == 1, h, t_a, t_b, qs, gs, C)
        else:
            place(p, core, h, t_a, t_b, qs, gs, C)
        window = win_ref[h]
        near_stats = stats_of(p, stat_1, h, C)
        far_stats = stats_of(p, stat_2, h, N)
        lse, rowdot = (
            jnp.concatenate([x, y], axis=1) for x, y in zip(near_stats, far_stats)
        )
        here = pl.ds(pl.multiple_of(h * D, 16), D)
        if p.far:
            later_state = far_ref[here, :]
        else:
            later_state = (
                message_1[here, :].astype(f32)
                + jnp.where(goes_on, message_2[here, :].astype(f32), 0.0)
            ).astype(bf16)
        for r in range(2):
            rows = slice(r * L, (r + 1) * L)
            wide = C + N if (r == 1 or not p.merged) else C
            k, v = ks[rows, :], vs[rows, :]
            q, g = qs[0:wide, :], gs[0:wide, :]
            s_pos = lax.broadcasted_iota(jnp.int32, (L, 1), 0) + r * L
            t_pos = lax.broadcasted_iota(jnp.int32, (L, wide), 1) + C
            allowed = t_pos <= jnp.minimum(hi_s[rows, :], s_pos + window - 1)
            dk, dv = key_side(k, v, q, g, lse[:, :wide], rowdot[:, :wide], allowed, c2, scale)
            kf = k.astype(f32)
            uses = code_s[rows, :] == first_next
            phi_k = feature(kf).astype(bf16)
            grad_phi_k = jnp.where(uses, dot_t(v, later_state), 0.0)
            dks[h, rows, :] = (dk_i[h, rows, :] + dk + slope(kf) * grad_phi_k).astype(bf16)
            dvs[h, rows, :] = (
                dv_i[h, rows, :] + dv + jnp.where(uses, dot(phi_k, later_state), 0.0)
            ).astype(bf16)

    for h in range(p.half):
        for n, src in ((0, dks), (1, dvs)):
            keep[n, h] = src[h, pl.ds(pl.multiple_of(core * L, 16), L), :]
            send[n, h] = src[h, pl.ds(pl.multiple_of((1 - core) * L, 16), L), :]


def later_keys(p, core, windows, payloads, far_state):
    vmem = pl.BlockSpec(memory_space=pltpu.VMEM)
    smem = pl.BlockSpec(memory_space=pltpu.SMEM)
    half = jax.ShapeDtypeStruct((2, p.half, p.length, p.width), bf16)
    extra = [far_state] if p.far else []
    tile = pltpu.VMEM((p.chip, p.width), bf16)
    tall = pltpu.VMEM((p.chip + p.tail_fill, p.width), bf16)
    stat = pltpu.VMEM((p.stat_rows, p.width), f32)
    return pl.pallas_call(
        functools.partial(later_body, p),
        out_shape=[half, half],
        in_specs=[smem, smem] + [vmem] * (10 + len(extra)),
        out_specs=[vmem] * 2,
        scratch_shapes=[
            tile,
            tile,
            tall,
            tall,
            stat,
            stat,
            pltpu.VMEM((p.chip, 1), jnp.int32),
            pltpu.VMEM((p.chip, 1), f32),
            pltpu.VMEM((p.half, p.chip, p.width), bf16),
            pltpu.VMEM((p.half, p.chip, p.width), bf16),
        ],
        compiler_params=pltpu.CompilerParams(vmem_limit_bytes=40 << 20),
        name="later_keys",
    )(core, windows, *payloads, *extra)


def unpack_body(p, core_ref, keep, other, out_a, out_b, scratch):
    core = core_ref[0]
    for n, out in ((0, out_a), (1, out_b)):
        for h in range(p.half):
            scratch[core * p.half + h] = keep[n, h].astype(f32)
            scratch[(1 - core) * p.half + h] = other[n, h].astype(f32)
        out[...] = jnp.swapaxes(scratch[...], 0, 1).astype(bf16)


def unpack(p, core, keep, other):
    vmem = pl.BlockSpec(memory_space=pltpu.VMEM)
    out = jax.ShapeDtypeStruct((p.length, p.heads, p.width), bf16)
    return pl.pallas_call(
        functools.partial(unpack_body, p),
        out_shape=[out, out],
        in_specs=[pl.BlockSpec(memory_space=pltpu.SMEM), vmem, vmem],
        out_specs=[vmem, vmem],
        scratch_shapes=[pltpu.VMEM((p.heads, p.length, p.width), f32)],
        compiler_params=pltpu.CompilerParams(vmem_limit_bytes=40 << 20),
        name="unpack",
    )(core, keep, other)


def folded(session, state, backward):
    sessions = lax.all_gather(session, "ctx")
    states = lax.all_gather(state, "ctx")
    count = lax.axis_size("ctx")
    here = lax.axis_index("ctx")

    def one(hop, carry):
        held, total = carry
        source = count - 1 - hop if backward else hop
        new = lax.dynamic_index_in_dim(sessions, source, 0, False)
        first, last = new[0], new[1]
        part = lax.dynamic_index_in_dim(states, source, 0, False).astype(f32)
        entering, leaving = (last, first) if backward else (first, last)
        whole = jnp.logical_and(entering == held, entering == leaving)
        return leaving, part + jnp.where(whole, total, 0.0)

    steps = count - 1 - here if backward else here
    start = (jnp.zeros((), jnp.int32) - 1, jnp.zeros(state.shape, f32))
    return lax.fori_loop(0, steps, one, start)[1].astype(bf16)


def shards(p, queries, key_vectors, value_vectors, targets, token_weights, sessions, window_size):
    L = p.length
    chips = lax.axis_size("ctx")
    core_id = lax.axis_index("pair").astype(jnp.int32)
    core = core_id.reshape(1)
    windows = lax.dynamic_slice_in_dim(window_size, core_id * p.half, p.half)

    def move(x, target):
        pairs = []
        for c in range(chips):
            for i in range(2):
                to, j = target(c, i)
                if 0 <= to < chips:
                    pairs.append((2 * c + i, 2 * to + j))
        return lax.ppermute(x, AXES, pairs)

    packed = pack(
        p,
        core,
        queries,
        key_vectors,
        value_vectors,
        targets,
        token_weights.reshape(-1, LANES),
        sessions.reshape(-1, LANES),
    )
    kv_same, kv_cross, qg_same, qg_cross = packed[:4]
    kv_pair = move(kv_cross, lambda c, i: (c, 1 - i))
    qg_pair = move(qg_cross, lambda c, i: (c, 1 - i))
    kv_n_same = move(kv_same, lambda c, i: (c + 1, i))
    qg_n_same = move(qg_same, lambda c, i: (c - 1, i))
    kv_n_cross = move(kv_cross, lambda c, i: (c + 1, 1 - i))
    qg_n_cross = move(qg_cross, lambda c, i: (c - 1, 1 - i))
    if p.merged:
        tail_same, tail_cross = packed[4:]
        got_cross = move(tail_cross, lambda c, i: (c + 2, 0) if i == 1 else (c - 2, 1))
        got_same = move(tail_same, lambda c, i: (c + 2, 1) if i == 1 else (c - 2, 0))
        kv_t = qg_t = None
        kv_t = (got_cross, got_same)
        qg_t = (got_cross, got_same)
    else:
        kv_t = (
            move(kv_same, lambda c, i: (c + 2, i)),
            move(kv_cross, lambda c, i: (c + 2, 1 - i)),
        )
        qg_t = (
            move(qg_same, lambda c, i: (c - 2, i)),
            move(qg_cross, lambda c, i: (c - 2, 1 - i)),
        )

    far_before = far_after = None
    if p.far:
        ends = jnp.stack([sessions[0], sessions[-1]])
        both = lax.all_gather(ends, "pair")
        chip_ends = jnp.stack([both[0, 0], both[1, 1]])
        own = kv_same[: p.rows - EXTRA].reshape(p.half, 2, L, p.width)
        pair = kv_pair[: p.rows - EXTRA].reshape(p.half, 2, L, p.width)
        all_sessions = lax.all_gather(sessions, "pair")
        keys_of = []
        total = jnp.zeros((p.half, p.width, p.width), f32)
        for part, owner in ((own, core_id), (pair, 1 - core_id)):
            rows = lax.dynamic_index_in_dim(all_sessions, owner, 0, False)
            phi = feature(part[:, 0].astype(f32))
            phi = jnp.where((rows == chip_ends[1])[None, :, None], phi, 0.0).astype(bf16)
            total = total + jnp.einsum(
                "hsk,hsd->hkd", phi, part[:, 1], preferred_element_type=f32
            )
        far_before = folded(chip_ends, total.astype(bf16), False).reshape(-1, p.width)

    keep, send, grad_num, message = forward(
        p,
        core,
        windows,
        (kv_same, qg_same, kv_pair, qg_pair, kv_n_same, kv_n_cross) + kv_t,
        far_before,
    )
    message_1 = move(message, lambda c, i: (c - 1, i))
    message_2 = move(message, lambda c, i: (c - 2, i))
    other = move(send, lambda c, i: (c, 1 - i))
    if p.far:
        state = message[: p.state_rows].reshape(p.half, p.width, p.width)
        far_after = folded(chip_ends, state, True).reshape(-1, p.width)
    dk, dv = own_keys(p, core, windows, kv_same, qg_same, kv_pair, qg_pair, grad_num, message)
    attended, grad_queries = unpack(p, core, keep, other)
    keep, send = later_keys(
        p,
        core,
        windows,
        (kv_same, kv_pair, qg_n_same, qg_n_cross) + qg_t + (message_1, message_2, dk, dv),
        far_after,
    )
    other = move(send, lambda c, i: (c, 1 - i))
    grad_keys, grad_values = unpack(p, core, keep, other)
    return (attended, grad_queries, grad_keys, grad_values)


def solution(mesh):
    rows = P(("groups", "ctx", "pair"), "head", None)
    events = P(("groups", "ctx", "pair"))

    def run(queries, key_vectors, value_vectors, targets, token_weights, sessions, window_size):
        total = queries.shape[0] // mesh.shape["groups"]
        length = total // (mesh.shape["ctx"] * mesh.shape["pair"])
        heads = queries.shape[1] // mesh.shape["head"]
        p = Plan(length, heads, queries.shape[2], total)
        return jax.shard_map(
            functools.partial(shards, p),
            mesh=mesh,
            in_specs=(rows, rows, rows, rows, events, events, P("head")),
            out_specs=(rows, rows, rows, rows),
            check_vma=False,
        )(queries, key_vectors, value_vectors, targets, token_weights, sessions, window_size)

    return run
```

```python
import functools
import math

import jax
import jax.numpy as jnp
from jax import lax
from jax.experimental import pallas as pl
from jax.experimental.pallas import tpu as pltpu
from jax.sharding import PartitionSpec as P

WIN = 1024
SESSIONS = 6
EPSILON = 1e-06
MASKED = -1e30
AXES = ("ctx", "pair")
EXTRA = 16
LANES = 128
VMEM_LIMIT = 20 << 20

f32 = jnp.float32
bf16 = jnp.bfloat16


def dot(a, b):
    return lax.dot_general(a, b, (((1,), (0,)), ((), ())), preferred_element_type=f32)


def dot_t(a, b):
    return lax.dot_general(a, b, (((1,), (1,)), ((), ())), preferred_element_type=f32)


def t_dot(a, b):
    return lax.dot_general(a, b, (((0,), (0,)), ((), ())), preferred_element_type=f32)


def feature(x):
    return jnp.where(x > 0, x + 1.0, jnp.exp(jnp.minimum(x, 0.0)))


def slope(x):
    return jnp.where(x > 0, 1.0, jnp.exp(jnp.minimum(x, 0.0)))


def params(micros):
    return dict(
        compiler_params=pltpu.CompilerParams(vmem_limit_bytes=VMEM_LIMIT),
        cost_estimate=pl.CostEstimate(
            flops=int(micros * 1.15e9), bytes_accessed=int(micros * 1e6), transcendentals=0
        ),
    )


def row_of(column):
    n = column.shape[0]
    return jnp.concatenate(
        [
            jnp.transpose(jnp.broadcast_to(column[i : i + LANES], (LANES, LANES)))[0:1]
            for i in range(0, n, LANES)
        ],
        axis=1,
    )


def column_of(rows):
    return jnp.concatenate(
        [
            jnp.transpose(jnp.broadcast_to(rows[i : i + 1], (LANES, LANES)))[:, 0:1]
            for i in range(rows.shape[0])
        ],
        axis=0,
    )


class Plan:
    def __init__(self, length, heads, width, total):
        self.length = length
        self.heads = heads
        self.all = heads // 2
        self.groups = 2 if self.all % 2 == 0 else 1
        self.half = self.all // self.groups
        self.width = width
        self.chip = 2 * length
        longest = total // 3
        reach = min(WIN, longest) - 1
        tail = max(reach - self.chip, 0)
        self.far = longest - 1 > 2 * self.chip or longest - 1 > reach
        self.merged = tail <= length
        self.tail = -(-tail // 16) * 16 if self.merged else length
        self.tail_fill = length if self.merged else self.chip
        self.before = self.tail_fill + self.chip
        self.code_rows = length // LANES
        self.stat_rows = -(-(2 * self.half * self.chip // LANES) // 16) * 16
        self.state_rows = self.half * width
        self.rows = self.half * 2 * length + EXTRA
        self.tail_rows = self.all * 2 * self.tail + EXTRA
        self.far_refs = 2 if self.merged else 4
        self.first_near = 3 if self.merged else 1
        self.pair_rows = self.all * 4 * length + EXTRA


def pack_body(p, core_ref, q_ref, k_ref, v_ref, t_ref, w_ref, s_ref, *rest):
    number = (len(rest) - 4) // 2
    outs, staged = rest[:number], rest[number : 2 * number]
    scratch, landed, sems, out_sems = rest[2 * number :]
    core = core_ref[0]
    L = p.length
    copies = [
        pltpu.make_async_copy(ref, landed.at[n], sems.at[n])
        for n, ref in enumerate((k_ref, v_ref, q_ref, t_ref))
    ]
    for copy in copies:
        copy.start()
    weight = column_of(w_ref[...].astype(f32))
    codes = jnp.concatenate(
        [s_ref[...].astype(f32) + 1.0, jnp.zeros((EXTRA - p.code_rows, LANES), f32)], axis=0
    ).astype(bf16)
    for ref in staged:
        ref[ref.shape[0] - EXTRA :, :] = codes
    for n in range(4):
        copies[n].wait()
        x = jnp.swapaxes(landed[n].astype(f32), 0, 1)
        if n == 3:
            x = x * weight[None]
        scratch[n] = x.astype(bf16)
    leaving = []

    def leave(n):
        leaving.append(pltpu.make_async_copy(staged[n], outs[n], out_sems.at[n]))
        leaving[-1].start()

    other = (1 - core) * p.all
    for n in range(4):
        for h in range(p.all):
            at = (n * p.all + h) * L
            staged[0][at : at + L, :] = scratch[n, other + h]
    leave(0)
    if p.merged:
        first = (1 - core) * 2
        lead = core * (L - p.tail)
        for t, base in ((1, core * p.all), (2, other)):
            for n in range(2):
                for h in range(p.all):
                    at = (n * p.all + h) * p.tail
                    staged[t][at : at + p.tail, :] = scratch[
                        first + n, base + h, pl.ds(pl.multiple_of(lead, 16), p.tail), :
                    ]
            leave(t)
    for g in range(p.groups):
        for x, first, base in (
            (0, core * 2, core * p.all),
            (1, (1 - core) * 2, core * p.all),
            (2, core * 2, other),
            (3, (1 - core) * 2, other),
        ):
            to = p.first_near + 4 * g + x
            for n in range(2):
                for h in range(p.half):
                    at = (n * p.half + h) * L
                    staged[to][at : at + L, :] = scratch[first + n, base + g * p.half + h]
            leave(to)
    for copy in leaving:
        copy.wait()


def pack(p, core, q, k, v, targets, weights, sessions):
    shapes = [(p.pair_rows, p.width)]
    if p.merged:
        shapes += [(p.tail_rows, p.width)] * 2
    shapes += [(p.rows, p.width)] * (4 * p.groups)
    vmem = pl.BlockSpec(memory_space=pltpu.VMEM)
    hbm = pl.BlockSpec(memory_space=pl.ANY)
    return pl.pallas_call(
        functools.partial(pack_body, p),
        out_shape=[jax.ShapeDtypeStruct(x, bf16) for x in shapes],
        in_specs=[pl.BlockSpec(memory_space=pltpu.SMEM)] + [hbm] * 4 + [vmem] * 2,
        out_specs=[hbm] * len(shapes),
        scratch_shapes=[pltpu.VMEM(x, bf16) for x in shapes]
        + [
            pltpu.VMEM((4, p.heads, p.length, p.width), bf16),
            pltpu.VMEM((4, p.length, p.heads, p.width), bf16),
            pltpu.SemaphoreType.DMA((4,)),
            pltpu.SemaphoreType.DMA((len(shapes),)),
        ],
        compiler_params=pltpu.CompilerParams(vmem_limit_bytes=56 << 20),
        name="pack",
    )(core, q, k, v, targets, weights, sessions)


def code_block(p, core, pick):
    one, two = (ref[ref.shape[0] - EXTRA :, :].astype(f32)[: p.code_rows] for ref in pick)
    return jnp.where(core == 0, one, two)


def count(condition):
    return jnp.sum(
        jnp.sum(jnp.where(condition, 1.0, 0.0), axis=1, keepdims=True), axis=0, keepdims=True
    )


def drive(streams):
    streams = list(streams)
    while streams:
        streams = [x for x in streams if next(x, streams) is not streams]


def flat(rows):
    return jnp.concatenate([rows[i : i + 1] for i in range(rows.shape[0])], axis=1)


def in_order(core, same, cross):
    first = jnp.where(core == 0, same, cross)
    second = jnp.where(core == 0, cross, same)
    return jnp.concatenate([first, second], axis=0)


class Chip:
    def __init__(self, p, core, same, cross):
        self.p, self.core, self.same, self.cross = p, core, same, cross

    def codes(self):
        return in_order(
            self.core,
            code_block(self.p, self.core, self.same),
            code_block(self.p, self.core, self.cross),
        )

    def bring(self, targets, start, index=None):
        p = self.p
        L = p.length
        for me in range(2):

            @pl.when(self.core == me)
            def _():
                for ref, which, lead in (
                    (self.same[me], me, None),
                    (self.cross[me], 1 - me, index),
                ):
                    to = start + which * L
                    for n, target in enumerate(targets):
                        for h in range(p.half):
                            at = n * p.half + h
                            if lead is not None:
                                at = (lead[0] + n) * p.all + lead[1] + h
                            target[h, to : to + L, :] = ref[at * L : (at + 1) * L, :]


def bring_tail(p, core, group, pick, targets, start):
    for me in range(2):

        @pl.when(core == me)
        def _():
            for n, target in enumerate(targets):
                for h in range(p.half):
                    at = (n * p.all + group * p.half + h) * p.tail
                    target[h, start : start + p.tail, :] = pick[me][at : at + p.tail, :]


def forward_body(p, group, core_ref, win_ref, *refs):
    (pair, x1, x2, r1, r2, r3, r4), refs = refs[:7], refs[7:]
    far, refs = refs[: p.far_refs], refs[p.far_refs :]
    if p.far:
        far_ref, refs = refs[0], refs[1:]
    att_keep, att_send, gn_out, message, ks, vs, qs, gs, atts, dqs, stat = refs
    core = core_ref[0]
    L, C, B, D = p.length, p.chip, p.before, p.width
    scale = 1.0 / math.sqrt(D)
    c2 = scale * math.log2(math.e)

    head = group * p.half
    own_keys_at = Chip(p, core, (x1, x2), (pair, pair))
    own_queries_at = Chip(p, core, (x2, x1), (pair, pair))
    near_at = Chip(p, core, (r1, r2), (r4, r3))
    own_keys_at.bring((ks, vs), B, (0, head))
    own_queries_at.bring((qs, gs), 0, (2, head))
    near_at.bring((ks, vs), p.tail_fill)
    own_codes = own_keys_at.codes()
    near_codes = near_at.codes()
    if p.merged:
        pick = (far[1], far[0])
        bring_tail(p, core, group, pick, (ks, vs), p.tail_fill - p.tail)
        far_codes = code_block(p, core, pick)
    else:
        far_at = Chip(p, core, (far[0], far[1]), (far[3], far[2]))
        far_at.bring((ks, vs), 0)
        far_codes = far_at.codes()
    halo_codes = jnp.concatenate([far_codes, near_codes], axis=0)
    code = column_of(own_codes)
    last = near_codes[2 * p.code_rows - 1 :, LANES - 1 :]
    first_own = own_codes[0:1, 0:1]
    lo_all = jnp.zeros((C, 1), f32)
    for n in range(1, SESSIONS + 1):
        start = count(own_codes < n) - count(halo_codes >= n)
        lo_all = jnp.where(code == n, start, lo_all)
    lo_all = lo_all.astype(jnp.int32)
    cont = count(jnp.logical_and(halo_codes == last, halo_codes > 0)).astype(jnp.int32)
    halo_pos = lax.broadcasted_iota(jnp.int32, (B, 1), 0) - B
    in_start = jnp.broadcast_to(halo_pos >= -cont, (B, D))
    if p.merged and p.tail < p.tail_fill:
        gap = p.tail_fill - p.tail
        ks[:, 0:gap, :] = jnp.zeros((p.half, gap, D), bf16)
        vs[:, 0:gap, :] = jnp.zeros((p.half, gap, D), bf16)
    phis, starts, states = {}, {}, {}

    def stream(h, r):
        rows = slice(r * L, (r + 1) * L)
        q = qs[h, rows, :]
        g = gs[h, rows, :]
        gf = g.astype(f32)
        qf = q.astype(f32)
        lo = lo_all[rows]
        mine = code[rows]
        t_pos = lax.broadcasted_iota(jnp.int32, (L, 1), 0) + r * L
        window = win_ref[core * p.all + group * p.half + h]
        begin = 0 if not p.merged else r * L
        n_halo = B - begin
        n_own = (r + 1) * L
        wide = n_halo + n_own
        low = jnp.maximum(lo, t_pos - window + 1)
        score = dot_t(q, ks[h, begin : begin + wide, :])
        yield
        if r == 0:
            phis[h] = feature(ks[h, B:, :].astype(f32)).astype(bf16)
            if p.far:
                starts[h] = far_ref[h * D : (h + 1) * D, :]
            else:
                halo_phi = jnp.where(in_start, feature(ks[h, 0:B, :].astype(f32)), 0.0)
                starts[h] = t_dot(halo_phi.astype(bf16), vs[h, 0:B, :]).astype(bf16)
        phi_k, start_state = phis[h], starts[h]
        phi_q = feature(qf).astype(bf16)
        a = dot_t(phi_q, phi_k[:n_own])
        from_start = dot(phi_q, start_state)
        yield
        s_pos = lax.broadcasted_iota(jnp.int32, (L, wide), 1) + (begin - B)
        own_pos = lax.broadcasted_iota(jnp.int32, (L, n_own), 1)
        causal = own_pos <= t_pos
        score = jnp.concatenate(
            [
                jnp.where(s_pos[:, :n_halo] >= low, score[:, :n_halo], MASKED),
                jnp.where(
                    jnp.logical_and(own_pos >= low, causal), score[:, n_halo:], MASKED
                ),
            ],
            axis=1,
        )
        peak = jnp.max(score, axis=1, keepdims=True) * c2
        e = jnp.exp2(score * c2 - peak)
        total = jnp.sum(e, axis=1, keepdims=True)
        yield
        inverse = 1.0 / total
        window_out = dot(e.astype(bf16), vs[h, begin : begin + wide, :]) * inverse
        alike = jnp.logical_and(own_pos >= lo, causal)
        a = jnp.where(alike, a, 0.0).astype(bf16)
        reads = mine == last
        numerator = dot(a, vs[h, B : B + n_own, :]) + jnp.where(reads, from_start, 0.0)
        grad_prob = dot_t(g, vs[h, begin : begin + wide, :])
        yield
        rowdot = jnp.sum(gf * window_out, axis=1, keepdims=True)
        inverse_rms = lax.rsqrt(jnp.mean(numerator * numerator, axis=1, keepdims=True) + EPSILON)
        linear_out = numerator * inverse_rms
        grad_num = (
            inverse_rms * (gf - linear_out * jnp.mean(gf * linear_out, axis=1, keepdims=True))
        ).astype(bf16)
        gn_out[h, rows, :] = grad_num
        atts[h, rows, :] = (linear_out + window_out).astype(bf16)
        b = dot_t(grad_num, vs[h, B : B + n_own, :])
        ds = (e * (grad_prob - rowdot)).astype(bf16)
        yield
        dq = dot(ds, ks[h, begin : begin + wide, :]) * (inverse * scale)
        opening = mine == first_own
        part = t_dot(jnp.where(opening, phi_q, jnp.zeros_like(phi_q)), grad_num)
        lse = peak + jnp.log2(total)
        for which, column in ((0, lse), (1, rowdot)):
            base = (which * p.half + h) * (C // LANES) + r * (L // LANES)
            row = row_of(column)
            for j in range(L // LANES):
                stat[base + j : base + j + 1, :] = row[:, j * LANES : (j + 1) * LANES]
        yield
        b = jnp.where(alike, b, 0.0).astype(bf16)
        grad_phi_q = dot(b, phi_k[:n_own]) + jnp.where(
            reads, dot_t(grad_num, start_state), 0.0
        )
        dqs[h, rows, :] = (slope(qf) * grad_phi_q + dq).astype(bf16)
        states[h] = states[h] + part if r else part
        if r:
            message[h * D : (h + 1) * D, :] = states[h].astype(bf16)

    drive(stream(h, r) for h in range(p.half) for r in range(2))

    values = stat[...]
    if 2 * p.half * C // LANES < p.stat_rows:
        used = lax.broadcasted_iota(jnp.int32, values.shape, 0) < 2 * p.half * C // LANES
        values = jnp.where(used, values, 0.0)
    for n in range(3):
        piece = values.astype(bf16)
        at = p.state_rows + n * p.stat_rows
        message[at : at + p.stat_rows, :] = piece
        values = values - piece.astype(f32)
    for h in range(p.half):
        for n, src in ((0, atts), (1, dqs)):
            att_keep[n, h] = src[h, pl.ds(pl.multiple_of(core * L, 16), L), :]
            att_send[n, h] = src[h, pl.ds(pl.multiple_of((1 - core) * L, 16), L), :]


def forward(p, group, core, windows, payloads, far_state):
    vmem = pl.BlockSpec(memory_space=pltpu.VMEM)
    smem = pl.BlockSpec(memory_space=pltpu.SMEM)
    half = jax.ShapeDtypeStruct((2, p.half, p.length, p.width), bf16)
    outs = [
        half,
        half,
        jax.ShapeDtypeStruct((p.half, p.chip, p.width), bf16),
        jax.ShapeDtypeStruct((p.state_rows + 3 * p.stat_rows, p.width), bf16),
    ]
    extra = [far_state] if p.far else []
    span = p.before + p.chip
    return pl.pallas_call(
        functools.partial(forward_body, p, group),
        out_shape=outs,
        in_specs=[smem, smem] + [vmem] * (7 + p.far_refs + len(extra)),
        out_specs=[vmem] * 4,
        scratch_shapes=[
            pltpu.VMEM((p.half, span, p.width), bf16),
            pltpu.VMEM((p.half, span, p.width), bf16),
            pltpu.VMEM((p.half, p.chip, p.width), bf16),
            pltpu.VMEM((p.half, p.chip, p.width), bf16),
            pltpu.VMEM((p.half, p.chip, p.width), bf16),
            pltpu.VMEM((p.half, p.chip, p.width), bf16),
            pltpu.VMEM((p.stat_rows, p.width), f32),
        ],
        **params(3 * p.half),
        name="forward",
    )(core, windows, *payloads, *extra)


def stats_of(p, values, head, count):
    per = p.chip // LANES
    result = []
    for which in range(2):
        base = (which * p.half + head) * per
        result.append(flat(values[base : base + per])[:, :count])
    return result


def unpack_stats(p, message):
    total = jnp.zeros((p.stat_rows, LANES), f32)
    for n in reversed(range(3)):
        at = p.state_rows + n * p.stat_rows
        total = total + message[at : at + p.stat_rows, :].astype(f32)
    return total


def own_body(p, group, core_ref, win_ref, pair, x1, x2, gn, message, dk_o, dv_o, *s):
    ks, vs, qs, gs = s
    core = core_ref[0]
    L, C, D = p.length, p.chip, p.width
    scale = 1.0 / math.sqrt(D)
    c2 = scale * math.log2(math.e)
    head = group * p.half
    own_keys_at = Chip(p, core, (x1, x2), (pair, pair))
    own_keys_at.bring((ks, vs), 0, (0, head))
    Chip(p, core, (x2, x1), (pair, pair)).bring((qs, gs), 0, (2, head))
    own_codes = own_keys_at.codes()
    code = column_of(own_codes)
    hi_all = jnp.zeros((C, 1), f32)
    for n in range(1, SESSIONS + 1):
        hi_all = jnp.where(code == n, count(own_codes <= n) - 1.0, hi_all)
    hi_all = hi_all.astype(jnp.int32)
    stats = unpack_stats(p, message)

    def stream(h, r):
        window = win_ref[core * p.all + group * p.half + h]
        lse, rowdot = stats_of(p, stats, h, C)
        rows = slice(r * L, (r + 1) * L)
        after = slice(r * L, C)
        wide = C - r * L
        k, v = ks[h, rows, :], vs[h, rows, :]
        q, g = qs[h, after, :], gs[h, after, :]
        score = dot_t(k, q)
        grad_prob = dot_t(v, g)
        yield
        phi_q = feature(q.astype(f32)).astype(bf16)
        kf = k.astype(f32)
        grad_num = gn[h, after, :]
        a = dot_t(feature(kf).astype(bf16), phi_q)
        b = dot_t(v, grad_num)
        yield
        hi = hi_all[rows]
        s_pos = lax.broadcasted_iota(jnp.int32, (L, 1), 0) + r * L
        t_pos = lax.broadcasted_iota(jnp.int32, (L, wide), 1) + r * L
        alike = jnp.logical_and(t_pos >= s_pos, t_pos <= hi)
        allowed = jnp.logical_and(alike, t_pos < s_pos + window)
        prob = jnp.exp2(jnp.where(allowed, score * c2 - lse[:, after], MASKED))
        ds = (prob * (grad_prob - rowdot[:, after])).astype(bf16)
        yield
        dk = dot(ds, q) * scale
        dv = dot(prob.astype(bf16), g)
        a = jnp.where(alike, a, 0.0).astype(bf16)
        b = jnp.where(alike, b, 0.0).astype(bf16)
        yield
        dk_o[h, rows, :] = dk + slope(kf) * dot(b, phi_q)
        dv_o[h, rows, :] = dv + dot(a, grad_num)

    drive(stream(h, r) for h in range(p.half) for r in range(2))


def own_keys(p, group, core, windows, pair, x1, x2, gn, message):
    vmem = pl.BlockSpec(memory_space=pltpu.VMEM)
    smem = pl.BlockSpec(memory_space=pltpu.SMEM)
    full = jax.ShapeDtypeStruct((p.half, p.chip, p.width), f32)
    tile = pltpu.VMEM((p.half, p.chip, p.width), bf16)
    return pl.pallas_call(
        functools.partial(own_body, p, group),
        out_shape=[full, full],
        in_specs=[smem, smem] + [vmem] * 5,
        out_specs=[vmem] * 2,
        scratch_shapes=[tile] * 4,
        **params(1.5 * p.half),
        name="own_keys",
    )(core, windows, pair, x1, x2, gn, message)


def later_body(p, group, core_ref, win_ref, *refs):
    (pair, x1, x2, r1, r2, r3, r4), refs = refs[:7], refs[7:]
    far, refs = refs[: p.far_refs], refs[p.far_refs :]
    (message_1, message_2, dk_i, dv_i), refs = refs[:4], refs[4:]
    if p.far:
        far_ref, refs = refs[0], refs[1:]
    keep, send, ks, vs, qs, gs, dks, dvs = refs
    core = core_ref[0]
    L, C, D = p.length, p.chip, p.width
    N = p.tail_fill
    scale = 1.0 / math.sqrt(D)
    c2 = scale * math.log2(math.e)
    head = group * p.half
    own_keys_at = Chip(p, core, (x1, x2), (pair, pair))
    near_at = Chip(p, core, (r2, r1), (r3, r4))
    own_keys_at.bring((ks, vs), 0, (0, head))
    near_at.bring((qs, gs), 0)
    own_codes = own_keys_at.codes()
    near_codes = near_at.codes()
    if p.merged:
        pick = (far[0], far[1])
        bring_tail(p, core, group, pick, (qs, gs), C)
        far_codes = code_block(p, core, pick)
    else:
        far_at = Chip(p, core, (far[1], far[0]), (far[2], far[3]))
        far_at.bring((qs, gs), C)
        far_codes = far_at.codes()
    after_codes = jnp.concatenate([near_codes, far_codes], axis=0)
    code = column_of(own_codes)
    final = own_codes[2 * p.code_rows - 1 :, LANES - 1 :]
    hi_last = C - 1 + count(after_codes == final)
    hi_all = jnp.where(code == final, hi_last, -1.0).astype(jnp.int32)
    first_next = near_codes[0:1, 0:1]
    goes_on = jnp.logical_and(first_next > 0, first_next == far_codes[0:1, 0:1])
    stats_1 = unpack_stats(p, message_1)
    stats_2 = unpack_stats(p, message_2)
    if p.merged and p.tail < p.tail_fill:
        gap = p.tail_fill - p.tail
        qs[:, C + p.tail :, :] = jnp.zeros((p.half, gap, D), bf16)
        gs[:, C + p.tail :, :] = jnp.zeros((p.half, gap, D), bf16)
    def stream(h, r):
        window = win_ref[core * p.all + group * p.half + h]
        lse, rowdot = (
            jnp.concatenate([x, y], axis=1)
            for x, y in zip(stats_of(p, stats_1, h, C), stats_of(p, stats_2, h, N))
        )
        rows = slice(r * L, (r + 1) * L)
        wide = C + N if (r == 1 or not p.merged) else C
        k, v = ks[h, rows, :], vs[h, rows, :]
        q, g = qs[h, 0:wide, :], gs[h, 0:wide, :]
        score = dot_t(k, q)
        grad_prob = dot_t(v, g)
        yield
        if p.far:
            later_state = far_ref[h * D : (h + 1) * D, :]
        else:
            here = slice(h * D, (h + 1) * D)
            later_state = (
                message_1[here, :].astype(f32)
                + jnp.where(goes_on, message_2[here, :].astype(f32), 0.0)
            ).astype(bf16)
        kf = k.astype(f32)
        uses = code[rows] == first_next
        phi_k = feature(kf).astype(bf16)
        dk_lin = dot_t(v, later_state)
        dv_lin = dot(phi_k, later_state)
        yield
        s_pos = lax.broadcasted_iota(jnp.int32, (L, 1), 0) + r * L
        t_pos = lax.broadcasted_iota(jnp.int32, (L, wide), 1) + C
        allowed = t_pos <= jnp.minimum(hi_all[rows], s_pos + window - 1)
        prob = jnp.exp2(jnp.where(allowed, score * c2 - lse[:, :wide], MASKED))
        ds = (prob * (grad_prob - rowdot[:, :wide])).astype(bf16)
        yield
        dk = dot(ds, q) * scale
        dv = dot(prob.astype(bf16), g)
        yield
        dks[h, rows, :] = (
            dk_i[h, rows, :] + dk + slope(kf) * jnp.where(uses, dk_lin, 0.0)
        ).astype(bf16)
        dvs[h, rows, :] = (dv_i[h, rows, :] + dv + jnp.where(uses, dv_lin, 0.0)).astype(bf16)

    drive(stream(h, r) for h in range(p.half) for r in range(2))

    for h in range(p.half):
        for n, src in ((0, dks), (1, dvs)):
            keep[n, h] = src[h, pl.ds(pl.multiple_of(core * L, 16), L), :]
            send[n, h] = src[h, pl.ds(pl.multiple_of((1 - core) * L, 16), L), :]


def later_keys(p, group, core, windows, payloads, far_state):
    vmem = pl.BlockSpec(memory_space=pltpu.VMEM)
    smem = pl.BlockSpec(memory_space=pltpu.SMEM)
    half = jax.ShapeDtypeStruct((2, p.half, p.length, p.width), bf16)
    extra = [far_state] if p.far else []
    tile = pltpu.VMEM((p.half, p.chip, p.width), bf16)
    tall = pltpu.VMEM((p.half, p.chip + p.tail_fill, p.width), bf16)
    return pl.pallas_call(
        functools.partial(later_body, p, group),
        out_shape=[half, half],
        in_specs=[smem, smem] + [vmem] * (11 + p.far_refs + len(extra)),
        out_specs=[vmem] * 2,
        scratch_shapes=[tile, tile, tall, tall, tile, tile],
        **params(1.5 * p.half),
        name="later_keys",
    )(core, windows, *payloads, *extra)


def unpack_body(p, core_ref, *refs):
    parts, (out_a, out_b, scratch) = refs[: 2 * p.groups], refs[2 * p.groups :]
    core = core_ref[0]
    for n, out in ((0, out_a), (1, out_b)):
        for group in range(p.groups):
            for ref, which in ((parts[2 * group], core), (parts[2 * group + 1], 1 - core)):
                for h in range(p.half):
                    scratch[which * p.all + group * p.half + h] = ref[n, h].astype(f32)
        out[...] = jnp.swapaxes(scratch[...], 0, 1).astype(bf16)


def unpack(p, core, parts):
    vmem = pl.BlockSpec(memory_space=pltpu.VMEM)
    out = jax.ShapeDtypeStruct((p.length, p.heads, p.width), bf16)
    return pl.pallas_call(
        functools.partial(unpack_body, p),
        out_shape=[out, out],
        in_specs=[pl.BlockSpec(memory_space=pltpu.SMEM)] + [vmem] * (2 * p.groups),
        out_specs=[vmem, vmem],
        scratch_shapes=[pltpu.VMEM((p.heads, p.length, p.width), f32)],
        **params(1.4),
        name="unpack",
    )(core, *parts)


def folded(session, state, backward):
    sessions = lax.all_gather(session, "ctx")
    states = lax.all_gather(state, "ctx")
    count = lax.axis_size("ctx")
    here = lax.axis_index("ctx")

    def one(hop, carry):
        held, total = carry
        source = count - 1 - hop if backward else hop
        new = lax.dynamic_index_in_dim(sessions, source, 0, False)
        first, last = new[0], new[1]
        part = lax.dynamic_index_in_dim(states, source, 0, False).astype(f32)
        entering, leaving = (last, first) if backward else (first, last)
        whole = jnp.logical_and(entering == held, entering == leaving)
        return leaving, part + jnp.where(whole, total, 0.0)

    steps = count - 1 - here if backward else here
    start = (jnp.zeros((), jnp.int32) - 1, jnp.zeros(state.shape, f32))
    return lax.fori_loop(0, steps, one, start)[1].astype(bf16)


def shards(p, queries, key_vectors, value_vectors, targets, token_weights, sessions, window_size):
    L = p.length
    chips = lax.axis_size("ctx")
    core_id = lax.axis_index("pair").astype(jnp.int32)
    core = core_id.reshape(1)
    def move(x, target):
        pairs = []
        for c in range(chips):
            for i in range(2):
                to, j = target(c, i)
                if 0 <= to < chips:
                    pairs.append((2 * c + i, 2 * to + j))
        return lax.ppermute(x, AXES, pairs)

    packed = pack(
        p,
        core,
        queries,
        key_vectors,
        value_vectors,
        targets,
        token_weights.reshape(-1, LANES),
        sessions.reshape(-1, LANES),
    )
    def exchange(payloads, by):
        x1, x2, x3, x4 = payloads
        return (
            move(x1, lambda c, i: (c + by, 0) if i == 0 else (c - by, 1)),
            move(x2, lambda c, i: (c + by, 1) if i == 1 else (c - by, 0)),
            move(x3, lambda c, i: (c + by, 1) if i == 0 else (c - by, 0)),
            move(x4, lambda c, i: (c + by, 0) if i == 1 else (c - by, 1)),
        )

    near = [packed[p.first_near + 4 * g : p.first_near + 4 * g + 4] for g in range(p.groups)]
    pair = move(packed[0], lambda c, i: (c, 1 - i))
    got = [exchange(x, 1) for x in near]
    if p.merged:
        first_tail, second_tail, pair = lax.optimization_barrier((packed[1], packed[2], pair))
        tails = (
            move(first_tail, lambda c, i: (c + 2, 1) if i == 1 else (c - 2, 0)),
            move(second_tail, lambda c, i: (c + 2, 0) if i == 1 else (c - 2, 1)),
        )
        far = [tails] * p.groups
    else:
        far = [exchange(x, 2) for x in near]

    if p.far:
        both = lax.all_gather(sessions, "pair")
        chip_ends = jnp.stack([both[0, 0], both[1, -1]])

    query_parts, key_parts = [], []
    for group in range(p.groups):
        x1, x2 = near[group][:2]
        near_by = (pair, x1, x2) + got[group] + far[group]
        far_before = far_after = None
        if p.far:
            total = jnp.zeros((p.half, p.width, p.width), f32)
            keys_here = jnp.where(core_id == 0, x1, x2)[: p.rows - EXTRA].reshape(2, p.half, L, p.width)
            keys_pair = pair[: p.pair_rows - EXTRA].reshape(4, p.all, L, p.width)
            keys_pair = keys_pair[:2, group * p.half : (group + 1) * p.half]
            for part, owner in ((keys_here, core_id), (keys_pair, 1 - core_id)):
                rows = lax.dynamic_index_in_dim(both, owner, 0, False)
                phi = feature(part[0].astype(f32))
                phi = jnp.where((rows == chip_ends[1])[None, :, None], phi, 0.0).astype(bf16)
                total = total + jnp.einsum(
                    "hsk,hsd->hkd", phi, part[1], preferred_element_type=f32
                )
            far_before = folded(chip_ends, total.astype(bf16), False).reshape(-1, p.width)
        keep, send, grad_num, message = forward(
            p,
            group,
            core,
            window_size,
            near_by,
            far_before,
        )
        message_1 = move(message, lambda c, i: (c - 1, i))
        message_2 = move(message, lambda c, i: (c - 2, i))
        query_parts += [keep, move(send, lambda c, i: (c, 1 - i))]
        if p.far:
            state = message[: p.state_rows].reshape(p.half, p.width, p.width)
            far_after = folded(chip_ends, state, True).reshape(-1, p.width)
        dk, dv = own_keys(p, group, core, window_size, pair, x1, x2, grad_num, message)
        keep, send = later_keys(
            p,
            group,
            core,
            window_size,
            near_by + (message_1, message_2, dk, dv),
            far_after,
        )
        key_parts += [keep, move(send, lambda c, i: (c, 1 - i))]
    attended, grad_queries = unpack(p, core, query_parts)
    grad_keys, grad_values = unpack(p, core, key_parts)
    return (attended, grad_queries, grad_keys, grad_values)


def solution(mesh):
    rows = P(("groups", "ctx", "pair"), "head", None)
    events = P(("groups", "ctx", "pair"))

    def run(queries, key_vectors, value_vectors, targets, token_weights, sessions, window_size):
        total = queries.shape[0] // mesh.shape["groups"]
        length = total // (mesh.shape["ctx"] * mesh.shape["pair"])
        heads = queries.shape[1] // mesh.shape["head"]
        p = Plan(length, heads, queries.shape[2], total)
        return jax.shard_map(
            functools.partial(shards, p),
            mesh=mesh,
            in_specs=(rows, rows, rows, rows, events, events, P("head")),
            out_specs=(rows, rows, rows, rows),
            check_vma=False,
        )(queries, key_vectors, value_vectors, targets, token_weights, sessions, window_size)

    return run
```

```python
import functools
import math

import jax
import jax.numpy as jnp
from jax import lax
from jax.experimental import pallas as pl
from jax.experimental.pallas import tpu as pltpu
from jax.sharding import PartitionSpec as P

WIN = 1024
SESSIONS = 6
EPSILON = 1e-06
MASKED = -1e30
AXES = ("ctx", "pair")
EXTRA = 16
LANES = 128
VMEM_LIMIT = 20 << 20

f32 = jnp.float32
bf16 = jnp.bfloat16


def dot(a, b):
    return lax.dot_general(a, b, (((1,), (0,)), ((), ())), preferred_element_type=f32)


def dot_t(a, b):
    return lax.dot_general(a, b, (((1,), (1,)), ((), ())), preferred_element_type=f32)


def t_dot(a, b):
    return lax.dot_general(a, b, (((0,), (0,)), ((), ())), preferred_element_type=f32)


def feature(x):
    return jnp.where(x > 0, x + 1.0, jnp.exp(jnp.minimum(x, 0.0)))


def slope(x):
    return jnp.where(x > 0, 1.0, jnp.exp(jnp.minimum(x, 0.0)))


def params(micros):
    return dict(
        compiler_params=pltpu.CompilerParams(vmem_limit_bytes=VMEM_LIMIT),
        cost_estimate=pl.CostEstimate(
            flops=int(micros * 1.15e9), bytes_accessed=int(micros * 1e6), transcendentals=0
        ),
    )


def row_of(column):
    n = column.shape[0]
    return jnp.concatenate(
        [
            jnp.transpose(jnp.broadcast_to(column[i : i + LANES], (LANES, LANES)))[0:1]
            for i in range(0, n, LANES)
        ],
        axis=1,
    )


def column_of(rows):
    return jnp.concatenate(
        [
            jnp.transpose(jnp.broadcast_to(rows[i : i + 1], (LANES, LANES)))[:, 0:1]
            for i in range(rows.shape[0])
        ],
        axis=0,
    )


class Plan:
    def __init__(self, length, heads, width, total):
        self.length = length
        self.heads = heads
        self.all = heads // 2
        self.width = width
        self.chip = 2 * length
        longest = total // 3
        reach = min(WIN, longest) - 1
        tail = max(reach - self.chip, 0)
        self.far = longest - 1 > 2 * self.chip or longest - 1 > reach
        self.merged = tail <= length
        self.tail = -(-tail // 16) * 16 if self.merged else length
        self.tail_fill = length if self.merged else self.chip
        self.before = self.tail_fill + self.chip
        self.code_rows = length // LANES
        self.rows = self.all * 2 * length + EXTRA
        self.tail_rows = self.all * 2 * self.tail + EXTRA
        self.pair_rows = self.all * 4 * length + EXTRA
        self.stat_rows = -(-2 * self.all * self.code_rows // 16) * 16
        self.state_rows = self.all * width
        self.far_refs = 2 if self.merged else 4


def pack_body(p, core_ref, q_ref, k_ref, v_ref, t_ref, w_ref, s_ref, *rest):
    number = (len(rest) - 4) // 2
    outs, staged = list(rest[:number]), list(rest[number : 2 * number])
    scratch, landed, sems, out_sems = rest[2 * number :]
    core = core_ref[0]
    L = p.length
    copies = [
        pltpu.make_async_copy(ref, landed.at[n], sems.at[n])
        for n, ref in enumerate((k_ref, v_ref, q_ref, t_ref))
    ]
    for copy_in in copies:
        copy_in.start()
    weight = column_of(w_ref[...].astype(f32))
    codes = jnp.concatenate(
        [s_ref[...].astype(f32) + 1.0, jnp.zeros((EXTRA - p.code_rows, LANES), f32)], axis=0
    ).astype(bf16)
    for ref in staged:
        ref[ref.shape[0] - EXTRA :, :] = codes
    leaving = []

    def leave():
        copy_out = pltpu.make_async_copy(staged.pop(0), outs.pop(0), out_sems.at[len(leaving)])
        copy_out.start()
        leaving.append(copy_out)

    other = (1 - core) * p.all
    for n in range(4):
        copies[n].wait()
        x = jnp.swapaxes(landed[n].astype(f32), 0, 1)
        if n == 3:
            x = x * weight[None]
        scratch[n] = x.astype(bf16)
    for n in range(4):
        for h in range(p.all):
            at = (n * p.all + h) * L
            staged[0][at : at + L, :] = scratch[n, other + h]
    leave()
    for first, base in (
        (core * 2, core * p.all),
        ((1 - core) * 2, core * p.all),
        (core * 2, other),
        ((1 - core) * 2, other),
    ):
        for n in range(2):
            for h in range(p.all):
                at = (n * p.all + h) * L
                staged[0][at : at + L, :] = scratch[first + n, base + h]
        leave()
    if p.merged:
        first = (1 - core) * 2
        lead = core * (L - p.tail)
        for base in (core * p.all, other):
            for n in range(2):
                for h in range(p.all):
                    at = (n * p.all + h) * p.tail
                    staged[0][at : at + p.tail, :] = scratch[
                        first + n, base + h, pl.ds(pl.multiple_of(lead, 16), p.tail), :
                    ]
            leave()
    for copy_out in leaving:
        copy_out.wait()


def pack(p, core, q, k, v, targets, weights, sessions):
    rows = [p.pair_rows] + [p.rows] * 4 + [p.tail_rows] * (2 if p.merged else 0)
    shapes = [(n, p.width) for n in rows]
    vmem = pl.BlockSpec(memory_space=pltpu.VMEM)
    hbm = pl.BlockSpec(memory_space=pl.ANY)
    return pl.pallas_call(
        functools.partial(pack_body, p),
        out_shape=[jax.ShapeDtypeStruct(x, bf16) for x in shapes],
        in_specs=[pl.BlockSpec(memory_space=pltpu.SMEM)] + [hbm] * 4 + [vmem] * 2,
        out_specs=[hbm] * len(shapes),
        scratch_shapes=[pltpu.VMEM(x, bf16) for x in shapes]
        + [
            pltpu.VMEM((4, p.heads, p.length, p.width), bf16),
            pltpu.VMEM((4, p.length, p.heads, p.width), bf16),
            pltpu.SemaphoreType.DMA((4,)),
            pltpu.SemaphoreType.DMA((len(shapes),)),
        ],
        compiler_params=pltpu.CompilerParams(vmem_limit_bytes=56 << 20),
        name="pack",
    )(core, q, k, v, targets, weights, sessions)


def code_block(p, core, pick):
    one, two = (ref[ref.shape[0] - EXTRA :, :].astype(f32)[: p.code_rows] for ref in pick)
    return jnp.where(core == 0, one, two)


def count(condition):
    return jnp.sum(
        jnp.sum(jnp.where(condition, 1.0, 0.0), axis=1, keepdims=True), axis=0, keepdims=True
    )


def drive(streams):
    streams = list(streams)
    while streams:
        streams = [x for x in streams if next(x, streams) is not streams]


def flat(rows):
    return jnp.concatenate([rows[i : i + 1] for i in range(rows.shape[0])], axis=1)


def in_order(core, same, cross):
    first = jnp.where(core == 0, same, cross)
    second = jnp.where(core == 0, cross, same)
    return jnp.concatenate([first, second], axis=0)


class Chip:
    def __init__(self, p, core, same, cross, index=0):
        self.p, self.core, self.same, self.cross = p, core, same, cross
        self.index = index

    def codes(self):
        return in_order(
            self.core,
            code_block(self.p, self.core, self.same),
            code_block(self.p, self.core, self.cross),
        )

    def bring(self, targets, start, tile=None):
        p = self.p
        L = p.length
        for me in range(2):

            @pl.when(self.core == me)
            def _():
                for ref, which, first in (
                    (self.same[me], me, 0),
                    (self.cross[me], 1 - me, self.index),
                ):
                    if tile not in (None, which):
                        continue
                    to = start + (which * L if tile is None else 0)
                    for n, target in enumerate(targets):
                        for h in range(p.all):
                            at = ((first + n) * p.all + h) * L
                            target[h, to : to + L, :] = ref[at : at + L, :]


def own_chip(p, core, refs):
    pair, x1, x2 = refs[:3]
    keys = Chip(p, core, (x1, x2), (pair, pair), 0)
    return keys, Chip(p, core, (x2, x1), (pair, pair), 2)


def near_chips(p, core, refs):
    r1, r2, r3, r4 = refs[3:7]
    return Chip(p, core, (r1, r2), (r4, r3)), Chip(p, core, (r2, r1), (r3, r4))


def bring_tail(p, core, pick, targets, start):
    for me in range(2):

        @pl.when(core == me)
        def _():
            for n, target in enumerate(targets):
                for h in range(p.all):
                    at = (n * p.all + h) * p.tail
                    target[h, start : start + p.tail, :] = pick[me][at : at + p.tail, :]


def divide(core, tiles, keep, send):
    for me in range(2):

        @pl.when(core == me)
        def _():
            keep[...] = tiles[me][...]
            send[...] = tiles[1 - me][...]


def forward_body(p, r, core_ref, win_ref, *refs):
    near, refs = refs[:7], refs[7:]
    far_here = r == 0 or not p.merged
    if far_here:
        far, refs = refs[: p.far_refs], refs[p.far_refs :]
    if p.far:
        far_ref, refs = refs[0], refs[1:]
    if r == 0:
        (state_in, stats_in, second), refs = refs[:3], refs[3:]
        keep, send, gn_out, stats_out, message, ks, vs, qs, gs, stat, out = refs
    else:
        out, gn_out, stats_out, state_out, ks, vs, qs, gs, stat = refs
    core = core_ref[0]
    L, C, B, D = p.length, p.chip, p.before, p.width
    scale = 1.0 / math.sqrt(D)
    c2 = scale * math.log2(math.e)

    own_keys_at, own_queries_at = own_chip(p, core, near)
    near_at, _ = near_chips(p, core, near)
    own_keys_at.bring((ks, vs), B)
    own_queries_at.bring((qs, gs), 0, r)
    near_at.bring((ks, vs), p.tail_fill)
    own_codes = own_keys_at.codes()
    near_codes = near_at.codes()
    halo_codes = near_codes
    if far_here:
        if p.merged:
            pick = (far[1], far[0])
            bring_tail(p, core, pick, (ks, vs), p.tail_fill - p.tail)
            far_codes = code_block(p, core, pick)
            if p.tail < p.tail_fill:
                gap = p.tail_fill - p.tail
                ks[:, 0:gap, :] = jnp.zeros((p.all, gap, D), bf16)
                vs[:, 0:gap, :] = jnp.zeros((p.all, gap, D), bf16)
        else:
            far_at = Chip(p, core, (far[0], far[1]), (far[3], far[2]))
            far_at.bring((ks, vs), 0)
            far_codes = far_at.codes()
        halo_codes = jnp.concatenate([far_codes, near_codes], axis=0)
    begin = 0 if far_here else p.tail_fill
    if not far_here:
        begin = max(begin, r * L)
    n_halo = B - begin
    n_own = (r + 1) * L
    wide = n_halo + n_own
    mine = column_of(own_codes[r * p.code_rows : (r + 1) * p.code_rows])
    last = near_codes[2 * p.code_rows - 1 :, LANES - 1 :]
    first_own = own_codes[0:1, 0:1]
    lo = jnp.zeros((L, 1), f32)
    for n in range(1, SESSIONS + 1):
        start = count(own_codes < n) - count(halo_codes >= n)
        lo = jnp.where(mine == n, start, lo)
    lo = lo.astype(jnp.int32)
    cont = count(jnp.logical_and(halo_codes == last, halo_codes > 0)).astype(jnp.int32)
    halo_pos = lax.broadcasted_iota(jnp.int32, (n_halo, 1), 0) - n_halo
    in_start = jnp.broadcast_to(halo_pos >= -cont, (n_halo, D))
    t_pos = lax.broadcasted_iota(jnp.int32, (L, 1), 0) + r * L
    reads = mine == last
    opening = mine == first_own

    def stream(h):
        q = qs[h]
        g = gs[h]
        gf = g.astype(f32)
        qf = q.astype(f32)
        window = win_ref[core * p.all + h]
        low = jnp.maximum(lo, t_pos - window + 1)
        k_part = ks[h, begin : begin + wide, :]
        v_part = vs[h, begin : begin + wide, :]
        v_own = vs[h, B : B + n_own, :]
        score = dot_t(q, k_part)
        yield
        phi_k = feature(ks[h, B : B + n_own, :].astype(f32)).astype(bf16)
        if p.far:
            start_state = far_ref[h * D : (h + 1) * D, :]
        else:
            halo_phi = jnp.where(in_start, feature(ks[h, begin:B, :].astype(f32)), 0.0)
            start_state = t_dot(halo_phi.astype(bf16), vs[h, begin:B, :]).astype(bf16)
        phi_q = feature(qf).astype(bf16)
        a = dot_t(phi_q, phi_k)
        from_start = dot(phi_q, start_state)
        yield
        s_pos = lax.broadcasted_iota(jnp.int32, (L, n_halo), 1) - n_halo
        own_pos = lax.broadcasted_iota(jnp.int32, (L, n_own), 1)
        causal = own_pos <= t_pos
        score = jnp.concatenate(
            [
                jnp.where(s_pos >= low, score[:, :n_halo], MASKED),
                jnp.where(
                    jnp.logical_and(own_pos >= low, causal), score[:, n_halo:], MASKED
                ),
            ],
            axis=1,
        )
        peak = jnp.max(score, axis=1, keepdims=True) * c2
        e = jnp.exp2(score * c2 - peak)
        total = jnp.sum(e, axis=1, keepdims=True)
        yield
        inverse = 1.0 / total
        window_out = dot(e.astype(bf16), v_part) * inverse
        alike = jnp.logical_and(own_pos >= lo, causal)
        a = jnp.where(alike, a, 0.0).astype(bf16)
        numerator = dot(a, v_own) + jnp.where(reads, from_start, 0.0)
        grad_prob = dot_t(g, v_part)
        yield
        rowdot = jnp.sum(gf * window_out, axis=1, keepdims=True)
        inverse_rms = lax.rsqrt(jnp.mean(numerator * numerator, axis=1, keepdims=True) + EPSILON)
        linear_out = numerator * inverse_rms
        grad_num = (
            inverse_rms * (gf - linear_out * jnp.mean(gf * linear_out, axis=1, keepdims=True))
        ).astype(bf16)
        gn_out[h] = grad_num
        out[0, h] = (linear_out + window_out).astype(bf16)
        b = dot_t(grad_num, v_own)
        ds = (e * (grad_prob - rowdot)).astype(bf16)
        yield
        dq = dot(ds, k_part) * (inverse * scale)
        state = t_dot(jnp.where(opening, phi_q, jnp.zeros_like(phi_q)), grad_num)
        lse = peak + jnp.log2(total)
        for which, column in ((0, lse), (1, rowdot)):
            base = (which * p.all + h) * p.code_rows
            row = row_of(column)
            for j in range(p.code_rows):
                stat[base + j : base + j + 1, :] = row[:, j * LANES : (j + 1) * LANES]
        yield
        b = jnp.where(alike, b, 0.0).astype(bf16)
        grad_phi_q = dot(b, phi_k) + jnp.where(reads, dot_t(grad_num, start_state), 0.0)
        out[1, h] = (slope(qf) * grad_phi_q + dq).astype(bf16)
        here = slice(h * D, (h + 1) * D)
        if r == 0:
            message[here, :] = (state_in[here, :] + state).astype(bf16)
        else:
            state_out[here, :] = state

    drive(stream(h) for h in range(p.all))

    if r == 0:
        divide(core, (out, second), keep, send)
    values = stat[...]
    used = 2 * p.all * p.code_rows
    if used < p.stat_rows:
        inside = lax.broadcasted_iota(jnp.int32, values.shape, 0) < used
        values = jnp.where(inside, values, 0.0)
    stats_out[...] = values
    if r == 0:
        for tile, values in enumerate((values, stats_in[...])):
            for n in range(3):
                piece = values.astype(bf16)
                at = p.state_rows + (3 * tile + n) * p.stat_rows
                message[at : at + p.stat_rows, :] = piece
                values = values - piece.astype(f32)


def forward(p, r, core, windows, near, far, far_state, carried=()):
    vmem = pl.BlockSpec(memory_space=pltpu.VMEM)
    smem = pl.BlockSpec(memory_space=pltpu.SMEM)
    both = jax.ShapeDtypeStruct((2, p.all, p.length, p.width), bf16)
    outs = [both] * (2 - r)
    outs += [
        jax.ShapeDtypeStruct((p.all, p.length, p.width), bf16),
        jax.ShapeDtypeStruct((p.stat_rows, p.width), f32),
    ]
    if r == 0:
        outs.append(jax.ShapeDtypeStruct((p.state_rows + 6 * p.stat_rows, p.width), bf16))
    else:
        outs.append(jax.ShapeDtypeStruct((p.state_rows, p.width), f32))
    args = list(near)
    if r == 0 or not p.merged:
        args += far
    if p.far:
        args.append(far_state)
    args += carried
    span = pltpu.VMEM((p.all, p.before + p.chip, p.width), bf16)
    tile = pltpu.VMEM((p.all, p.length, p.width), bf16)
    return pl.pallas_call(
        functools.partial(forward_body, p, r),
        out_shape=outs,
        in_specs=[smem, smem] + [vmem] * len(args),
        out_specs=[vmem] * len(outs),
        scratch_shapes=[span, span, tile, tile, pltpu.VMEM((p.stat_rows, p.width), f32)]
        + ([pltpu.VMEM(both.shape, bf16)] if r == 0 else []),
        **params(5.7),
        name="forward",
    )(core, windows, *args)


def stats_of(p, values, head):
    result = []
    for which in range(2):
        base = (which * p.all + head) * p.code_rows
        result.append(flat(values[base : base + p.code_rows]))
    return result


def unpack_stats(p, message, tile):
    total = jnp.zeros((p.stat_rows, LANES), f32)
    for n in reversed(range(3)):
        at = p.state_rows + (3 * tile + n) * p.stat_rows
        total = total + message[at : at + p.stat_rows, :].astype(f32)
    return total


def own_body(p, r, core_ref, win_ref, *refs):
    near, (gn, stats_in), refs = refs[:3], refs[3:5], refs[5:]
    if r == 0:
        (dk_i, dv_i), refs = refs[:2], refs[2:]
    dk_o, dv_o, ks, vs, qs, gs = refs
    core = core_ref[0]
    L, C, D = p.length, p.chip, p.width
    scale = 1.0 / math.sqrt(D)
    c2 = scale * math.log2(math.e)
    own_keys_at, own_queries_at = own_chip(p, core, near)
    own_keys_at.bring((ks, vs), 0)
    own_queries_at.bring((qs, gs), 0, r)
    own_codes = own_keys_at.codes()
    code = column_of(own_codes)
    hi_all = jnp.zeros((C, 1), f32)
    for n in range(1, SESSIONS + 1):
        hi_all = jnp.where(code == n, count(own_codes <= n) - 1.0, hi_all)
    hi_all = hi_all.astype(jnp.int32)
    stats = stats_in[...]

    def stream(h, tile):
        window = win_ref[core * p.all + h]
        lse, rowdot = stats_of(p, stats, h)
        rows = slice(tile * L, (tile + 1) * L)
        k, v = ks[h, rows, :], vs[h, rows, :]
        q, g = qs[h], gs[h]
        score = dot_t(k, q)
        grad_prob = dot_t(v, g)
        yield
        phi_q = feature(q.astype(f32)).astype(bf16)
        kf = k.astype(f32)
        grad_num = gn[h]
        a = dot_t(feature(kf).astype(bf16), phi_q)
        b = dot_t(v, grad_num)
        yield
        hi = hi_all[rows]
        s_pos = lax.broadcasted_iota(jnp.int32, (L, 1), 0) + tile * L
        t_pos = lax.broadcasted_iota(jnp.int32, (L, L), 1) + r * L
        alike = t_pos <= hi
        if tile == r:
            alike = jnp.logical_and(alike, t_pos >= s_pos)
        allowed = jnp.logical_and(alike, t_pos < s_pos + window)
        prob = jnp.exp2(jnp.where(allowed, score * c2 - lse, MASKED))
        ds = (prob * (grad_prob - rowdot)).astype(bf16)
        yield
        dk = dot(ds, q) * scale
        dv = dot(prob.astype(bf16), g)
        a = jnp.where(alike, a, 0.0).astype(bf16)
        b = jnp.where(alike, b, 0.0).astype(bf16)
        yield
        dk = dk + slope(kf) * dot(b, phi_q)
        dv = dv + dot(a, grad_num)
        if r == 0:
            dk_o[h] = dk_i[h, rows, :] + dk
            dv_o[h] = dv_i[h, rows, :] + dv
        else:
            dk_o[h, rows, :] = dk
            dv_o[h, rows, :] = dv

    drive(stream(h, tile) for h in range(p.all) for tile in range(r + 1))


def own_keys(p, r, core, windows, near, gn, stats, carried=()):
    vmem = pl.BlockSpec(memory_space=pltpu.VMEM)
    smem = pl.BlockSpec(memory_space=pltpu.SMEM)
    full = jax.ShapeDtypeStruct((p.all, p.chip if r else p.length, p.width), f32)
    args = [*near[:3], gn, stats, *carried]
    keys = pltpu.VMEM((p.all, p.chip, p.width), bf16)
    tile = pltpu.VMEM((p.all, p.length, p.width), bf16)
    return pl.pallas_call(
        functools.partial(own_body, p, r),
        out_shape=[full, full],
        in_specs=[smem, smem] + [vmem] * len(args),
        out_specs=[vmem] * 2,
        scratch_shapes=[keys, keys, tile, tile],
        **params(4.0 if r else 2.0),
        name="own_keys",
    )(core, windows, *args)


def later_body(p, core_ref, win_ref, *refs):
    near, refs = refs[:7], refs[7:]
    far, refs = refs[: p.far_refs], refs[p.far_refs :]
    (message_1, message_2), sums, refs = refs[:2], (refs[2:4], refs[4:6]), refs[6:]
    if p.far:
        far_ref, refs = refs[0], refs[1:]
    keep, send, ks, vs, qs, gs, first, second = refs
    core = core_ref[0]
    L, C, D = p.length, p.chip, p.width
    N = p.tail_fill
    scale = 1.0 / math.sqrt(D)
    c2 = scale * math.log2(math.e)
    own_keys_at, _ = own_chip(p, core, near)
    _, near_at = near_chips(p, core, near)
    own_keys_at.bring((ks, vs), 0)
    near_at.bring((qs, gs), 0)
    own_codes = own_keys_at.codes()
    near_codes = near_at.codes()
    if p.merged:
        pick = (far[0], far[1])
        far_codes = code_block(p, core, pick)
        bring_tail(p, core, pick, (qs, gs), C)
        if p.tail < p.tail_fill:
            gap = p.tail_fill - p.tail
            qs[:, C + p.tail :, :] = jnp.zeros((p.all, gap, D), bf16)
            gs[:, C + p.tail :, :] = jnp.zeros((p.all, gap, D), bf16)
    else:
        far_at = Chip(p, core, (far[1], far[0]), (far[2], far[3]))
        far_at.bring((qs, gs), C)
        far_codes = far_at.codes()
    after_codes = jnp.concatenate([near_codes, far_codes], axis=0)
    code = column_of(own_codes)
    final = own_codes[2 * p.code_rows - 1 :, LANES - 1 :]
    hi_last = C - 1 + count(after_codes == final)
    hi = jnp.where(code == final, hi_last, -1.0).astype(jnp.int32)
    first_next = near_codes[0:1, 0:1]
    goes_on = jnp.logical_and(first_next > 0, first_next == far_codes[0:1, 0:1])
    tiles = [unpack_stats(p, message_1, 0), unpack_stats(p, message_1, 1)]
    tiles += [unpack_stats(p, message_2, n) for n in range(N // L)]

    def stream(h, r):
        far_here = r == 1 or not p.merged
        wide = C + N if far_here else C
        rows = slice(r * L, (r + 1) * L)
        uses = code[rows] == first_next
        dk_i, dv_i = sums[r]
        window = win_ref[core * p.all + h]
        lse, rowdot = (
            jnp.concatenate(x, axis=1) for x in zip(*(stats_of(p, tile, h) for tile in tiles[: wide // L]))
        )
        k, v = ks[h, rows, :], vs[h, rows, :]
        q, g = qs[h, 0:wide, :], gs[h, 0:wide, :]
        score = dot_t(k, q)
        grad_prob = dot_t(v, g)
        yield
        here = slice(h * D, (h + 1) * D)
        if p.far:
            later_state = far_ref[here, :]
        else:
            later_state = message_1[here, :]
            if far_here:
                later_state = (
                    later_state.astype(f32)
                    + jnp.where(goes_on, message_2[here, :].astype(f32), 0.0)
                ).astype(bf16)
        kf = k.astype(f32)
        phi_k = feature(kf).astype(bf16)
        dk_lin = dot_t(v, later_state)
        dv_lin = dot(phi_k, later_state)
        yield
        s_pos = lax.broadcasted_iota(jnp.int32, (L, 1), 0) + r * L
        t_pos = lax.broadcasted_iota(jnp.int32, (L, wide), 1) + C
        allowed = t_pos <= jnp.minimum(hi[rows], s_pos + window - 1)
        prob = jnp.exp2(jnp.where(allowed, score * c2 - lse, MASKED))
        ds = (prob * (grad_prob - rowdot)).astype(bf16)
        yield
        dk = dot(ds, q) * scale
        dv = dot(prob.astype(bf16), g)
        yield
        out = (first, second)[r]
        dk = dk_i[h, rows, :] + dk + slope(kf) * jnp.where(uses, dk_lin, 0.0)
        dv = dv_i[h, rows, :] + dv + jnp.where(uses, dv_lin, 0.0)
        out[0, h] = dk.astype(bf16)
        out[1, h] = dv.astype(bf16)

    drive(stream(h, r) for h in range(p.all) for r in range(2))
    divide(core, (first, second), keep, send)


def later_keys(p, core, windows, near, far, messages, sums, far_state):
    vmem = pl.BlockSpec(memory_space=pltpu.VMEM)
    smem = pl.BlockSpec(memory_space=pltpu.SMEM)
    args = [*near, *far, *messages, *sums] + ([far_state] if p.far else [])
    both = jax.ShapeDtypeStruct((2, p.all, p.length, p.width), bf16)
    keys = pltpu.VMEM((p.all, p.chip, p.width), bf16)
    tall = pltpu.VMEM((p.all, p.chip + p.tail_fill, p.width), bf16)
    return pl.pallas_call(
        functools.partial(later_body, p),
        out_shape=[both, both],
        in_specs=[smem, smem] + [vmem] * len(args),
        out_specs=[vmem, vmem],
        scratch_shapes=[keys, keys, tall, tall] + [pltpu.VMEM(both.shape, bf16)] * 2,
        **params(5.5),
        name="later_keys",
    )(core, windows, *args)


def unpack_body(p, core_ref, mine, theirs, out_a, out_b, scratch):
    core = core_ref[0]
    for n in range(2):
        for h in range(p.all):
            scratch[n, core * p.all + h] = mine[n, h].astype(f32)
            scratch[n, (1 - core) * p.all + h] = theirs[n, h].astype(f32)
    for n, out in ((0, out_a), (1, out_b)):
        out[...] = jnp.swapaxes(scratch[n], 0, 1).astype(bf16)


def unpack(p, core, mine, theirs):
    vmem = pl.BlockSpec(memory_space=pltpu.VMEM)
    out = jax.ShapeDtypeStruct((p.length, p.heads, p.width), bf16)
    return pl.pallas_call(
        functools.partial(unpack_body, p),
        out_shape=[out, out],
        in_specs=[pl.BlockSpec(memory_space=pltpu.SMEM)] + [vmem] * 2,
        out_specs=[vmem, vmem],
        scratch_shapes=[pltpu.VMEM((2, p.heads, p.length, p.width), f32)],
        **params(1.4),
        name="unpack",
    )(core, mine, theirs)


def folded(session, state, backward):
    sessions = lax.all_gather(session, "ctx")
    states = lax.all_gather(state, "ctx")
    count = lax.axis_size("ctx")
    here = lax.axis_index("ctx")

    def one(hop, carry):
        held, total = carry
        source = count - 1 - hop if backward else hop
        new = lax.dynamic_index_in_dim(sessions, source, 0, False)
        first, last = new[0], new[1]
        part = lax.dynamic_index_in_dim(states, source, 0, False).astype(f32)
        entering, leaving = (last, first) if backward else (first, last)
        whole = jnp.logical_and(entering == held, entering == leaving)
        return leaving, part + jnp.where(whole, total, 0.0)

    steps = count - 1 - here if backward else here
    start = (jnp.zeros((), jnp.int32) - 1, jnp.zeros(state.shape, f32))
    return lax.fori_loop(0, steps, one, start)[1].astype(bf16)


def shards(p, queries, key_vectors, value_vectors, targets, token_weights, sessions, window_size):
    L = p.length
    chips = lax.axis_size("ctx")
    core_id = lax.axis_index("pair").astype(jnp.int32)
    core = core_id.reshape(1)
    def move(x, target):
        pairs = []
        for c in range(chips):
            for i in range(2):
                to, j = target(c, i)
                if 0 <= to < chips:
                    pairs.append((2 * c + i, 2 * to + j))
        return lax.ppermute(x, AXES, pairs)

    packed = pack(
        p,
        core,
        queries,
        key_vectors,
        value_vectors,
        targets,
        token_weights.reshape(-1, LANES),
        sessions.reshape(-1, LANES),
    )
    for_pair, payloads, tails = packed[0], packed[1:5], packed[5:]

    def exchange(payloads, by):
        x1, x2, x3, x4 = payloads
        return (
            move(x1, lambda c, i: (c + by, 0) if i == 0 else (c - by, 1)),
            move(x2, lambda c, i: (c + by, 1) if i == 1 else (c - by, 0)),
            move(x3, lambda c, i: (c + by, 1) if i == 0 else (c - by, 0)),
            move(x4, lambda c, i: (c + by, 0) if i == 1 else (c - by, 1)),
        )

    pair = move(for_pair, lambda c, i: (c, 1 - i))
    got = exchange(payloads, 1)
    if p.merged:
        tail_1, r1 = lax.optimization_barrier((tails[0], got[0]))
        tail_2, r2 = lax.optimization_barrier((tails[1], got[1]))
        got = (r1, r2, *got[2:])
        far = (
            move(tail_1, lambda c, i: (c + 2, 1) if i == 1 else (c - 2, 0)),
            move(tail_2, lambda c, i: (c + 2, 0) if i == 1 else (c - 2, 1)),
        )
    else:
        far = exchange(payloads, 2)
    near = (pair, *payloads[:2], *got)

    far_before = far_after = None
    if p.far:
        both = lax.all_gather(sessions, "pair")
        chip_ends = jnp.stack([both[0, 0], both[1, -1]])

        total = jnp.zeros((p.all, p.width, p.width), f32)
        keys_here = jnp.where(core_id == 0, payloads[0], payloads[1])[: p.rows - EXTRA]
        keys_here = keys_here.reshape(2, p.all, L, p.width)
        keys_pair = pair[: p.pair_rows - EXTRA].reshape(4, p.all, L, p.width)[:2]
        for part, owner in ((keys_here, core_id), (keys_pair, 1 - core_id)):
            rows = lax.dynamic_index_in_dim(both, owner, 0, False)
            phi = feature(part[0].astype(f32))
            phi = jnp.where((rows == chip_ends[1])[None, :, None], phi, 0.0).astype(bf16)
            total = total + jnp.einsum(
                "hsk,hsd->hkd", phi, part[1], preferred_element_type=f32
            )
        far_before = folded(chip_ends, total.astype(bf16), False).reshape(-1, p.width)

    queries_1, grad_1, stats_1, state_1 = forward(p, 1, core, window_size, near, far, far_before)
    keep_q, send_q, grad_0, stats_0, message = forward(
        p, 0, core, window_size, near, far, far_before, (state_1, stats_1, queries_1)
    )
    messages = (
        move(message, lambda c, i: (c - 1, i)),
        move(message, lambda c, i: (c - 2, i)),
    )
    if p.far:
        state = message[: p.state_rows].reshape(p.all, p.width, p.width)
        far_after = folded(chip_ends, state, True).reshape(-1, p.width)
    sums_1 = own_keys(p, 1, core, window_size, near, grad_1, stats_1)
    sums_0 = own_keys(p, 0, core, window_size, near, grad_0, stats_0, sums_1)
    keep_k, send_k = later_keys(
        p, core, window_size, near, far, messages, (*sums_0, *sums_1), far_after
    )
    attended, grad_queries = unpack(p, core, keep_q, move(send_q, lambda c, i: (c, 1 - i)))
    grad_keys, grad_values = unpack(p, core, keep_k, move(send_k, lambda c, i: (c, 1 - i)))
    return (attended, grad_queries, grad_keys, grad_values)


def solution(mesh):
    rows = P(("groups", "ctx", "pair"), "head", None)
    events = P(("groups", "ctx", "pair"))

    def run(queries, key_vectors, value_vectors, targets, token_weights, sessions, window_size):
        total = queries.shape[0] // mesh.shape["groups"]
        length = total // (mesh.shape["ctx"] * mesh.shape["pair"])
        heads = queries.shape[1] // mesh.shape["head"]
        p = Plan(length, heads, queries.shape[2], total)
        return jax.shard_map(
            functools.partial(shards, p),
            mesh=mesh,
            in_specs=(rows, rows, rows, rows, events, events, P("head")),
            out_specs=(rows, rows, rows, rows),
            check_vma=False,
        )(queries, key_vectors, value_vectors, targets, token_weights, sessions, window_size)

    return run
```

```python
import functools
import math

import jax
import jax.numpy as jnp
from jax import lax
from jax.experimental import pallas as pl
from jax.experimental.pallas import tpu as pltpu
from jax.sharding import PartitionSpec as P

WIN = 1024
SESSIONS = 6
EPSILON = 1e-06
MASKED = -1e30
AXES = ("ctx", "pair")
EXTRA = 16
LANES = 128
VMEM_LIMIT = 20 << 20

f32 = jnp.float32
bf16 = jnp.bfloat16


def dot(a, b):
    return lax.dot_general(a, b, (((1,), (0,)), ((), ())), preferred_element_type=f32)


def dot_t(a, b):
    return lax.dot_general(a, b, (((1,), (1,)), ((), ())), preferred_element_type=f32)


def t_dot(a, b):
    return lax.dot_general(a, b, (((0,), (0,)), ((), ())), preferred_element_type=f32)


def feature(x):
    return jnp.where(x > 0, x + 1.0, jnp.exp(jnp.minimum(x, 0.0)))


def slope(x):
    return jnp.where(x > 0, 1.0, jnp.exp(jnp.minimum(x, 0.0)))


def params(micros):
    return dict(
        compiler_params=pltpu.CompilerParams(vmem_limit_bytes=VMEM_LIMIT),
        cost_estimate=pl.CostEstimate(
            flops=int(micros * 1.15e9), bytes_accessed=int(micros * 1e6), transcendentals=0
        ),
    )


def row_of(column):
    n = column.shape[0]
    return jnp.concatenate(
        [
            jnp.transpose(jnp.broadcast_to(column[i : i + LANES], (LANES, LANES)))[0:1]
            for i in range(0, n, LANES)
        ],
        axis=1,
    )


def column_of(rows):
    return jnp.concatenate(
        [
            jnp.transpose(jnp.broadcast_to(rows[i : i + 1], (LANES, LANES)))[:, 0:1]
            for i in range(rows.shape[0])
        ],
        axis=0,
    )


class Plan:
    def __init__(self, length, heads, width, total):
        self.length = length
        self.heads = heads
        self.all = heads // 2
        self.width = width
        self.chip = 2 * length
        longest = total // 3
        reach = min(WIN, longest) - 1
        tail = max(reach - self.chip, 0)
        self.far = longest - 1 > 2 * self.chip or longest - 1 > reach
        self.merged = tail <= length
        self.tail = -(-tail // 16) * 16 if self.merged else length
        self.tail_fill = length if self.merged else self.chip
        self.before = self.tail_fill + self.chip
        self.code_rows = length // LANES
        self.rows = self.all * 2 * length + EXTRA
        self.tail_rows = self.all * 2 * self.tail + EXTRA
        self.pair_rows = self.all * 4 * length + EXTRA
        self.stat_rows = -(-2 * self.all * self.code_rows // 16) * 16
        self.state_rows = self.all * width
        self.far_refs = 1 if self.merged else 2


def pack_body(p, core_ref, q_ref, k_ref, v_ref, t_ref, w_ref, s_ref, *rest):
    number = (len(rest) - 3) // 2
    outs, staged = rest[:number], rest[number : 2 * number]
    landed, sems, out_sems = rest[2 * number :]
    L = p.length
    copies = [
        pltpu.make_async_copy(ref, landed.at[n], sems.at[n])
        for n, ref in enumerate((k_ref, v_ref, q_ref, t_ref))
    ]
    for copy_in in copies:
        copy_in.start()
    weight = column_of(w_ref[...].astype(f32))
    codes = jnp.concatenate(
        [s_ref[...].astype(f32) + 1.0, jnp.zeros((EXTRA - p.code_rows, LANES), f32)], axis=0
    ).astype(bf16)
    for ref in staged:
        ref[ref.shape[0] - EXTRA :, :] = codes

    def pack_for(me):
        leaving = []

        def leave(x, part, parts, rows):
            here = slice(part * rows, (part + 1) * rows + EXTRA * (part == parts - 1))
            copy_out = pltpu.make_async_copy(
                staged[x].at[here, :], outs[x].at[here, :], out_sems.at[len(leaving)]
            )
            copy_out.start()
            leaving.append(copy_out)

        for n in range(4):
            copies[n].wait()
            x = jnp.swapaxes(landed[n].astype(f32), 0, 1)
            if n == 3:
                x = x * weight[None]
            x = x.astype(bf16)
            mine = x[me * p.all : (me + 1) * p.all]
            other = x[(1 - me) * p.all : (2 - me) * p.all]
            to = n % 2 * p.all
            for at, heads in ((1 + n // 2 * 2, mine), (2 + n // 2 * 2, other)):
                for h in range(p.all):
                    staged[at][(to + h) * L : (to + h + 1) * L, :] = heads[h]
                leave(at, n % 2, 2, p.all * L)
            for h in range(p.all):
                staged[0][(n * p.all + h) * L : (n * p.all + h + 1) * L, :] = other[h]
            leave(0, n, 4, p.all * L)
        for copy_out in leaving:
            copy_out.wait()

    for me in range(2):

        @pl.when(core_ref[0] == me)
        def _():
            pack_for(me)


def pack(p, core, q, k, v, targets, weights, sessions):
    rows = [p.pair_rows] + [p.rows] * 4
    shapes = [(n, p.width) for n in rows]
    vmem = pl.BlockSpec(memory_space=pltpu.VMEM)
    hbm = pl.BlockSpec(memory_space=pl.ANY)
    return pl.pallas_call(
        functools.partial(pack_body, p),
        out_shape=[jax.ShapeDtypeStruct(x, bf16) for x in shapes],
        in_specs=[pl.BlockSpec(memory_space=pltpu.SMEM)] + [hbm] * 4 + [vmem] * 2,
        out_specs=[hbm] * len(shapes),
        scratch_shapes=[pltpu.VMEM(x, bf16) for x in shapes]
        + [
            pltpu.VMEM((4, p.length, p.heads, p.width), bf16),
            pltpu.SemaphoreType.DMA((4,)),
            pltpu.SemaphoreType.DMA((12,)),
        ],
        compiler_params=pltpu.CompilerParams(vmem_limit_bytes=56 << 20),
        name="pack",
    )(core, q, k, v, targets, weights, sessions)


def tails_body(p, core_ref, pair, own_keys, own_queries, keys, queries):
    L = p.length

    def tails_for(me):
        sources = [(pair, 0), (own_queries, 0)] if me == 0 else [(own_keys, 0), (pair, 2)]
        for out, (ref, first), lead in zip((keys, queries), sources, (L - p.tail, 0)):
            for n in range(2 * p.all):
                at = (first * p.all + n) * L + lead
                out[n * p.tail : (n + 1) * p.tail, :] = ref[at : at + p.tail, :]
            out[p.tail_rows - EXTRA :, :] = ref[ref.shape[0] - EXTRA :, :]

    for me in range(2):

        @pl.when(core_ref[0] == me)
        def _():
            tails_for(me)


def make_tails(p, core, pair, own_keys, own_queries):
    vmem = pl.BlockSpec(memory_space=pltpu.VMEM)
    out = jax.ShapeDtypeStruct((p.tail_rows, p.width), bf16)
    return pl.pallas_call(
        functools.partial(tails_body, p),
        out_shape=[out, out],
        in_specs=[pl.BlockSpec(memory_space=pltpu.SMEM), vmem, vmem, vmem],
        out_specs=[vmem, vmem],
        **params(1.0),
        name="tails",
    )(core, pair, own_keys, own_queries)


def code_block(p, ref):
    return ref[ref.shape[0] - EXTRA :, :].astype(f32)[: p.code_rows]


def count(condition):
    return jnp.sum(
        jnp.sum(jnp.where(condition, 1.0, 0.0), axis=1, keepdims=True), axis=0, keepdims=True
    )


def drive(streams):
    streams = list(streams)
    while streams:
        streams = [x for x in streams if next(x, streams) is not streams]


def flat(rows):
    return jnp.concatenate([rows[i : i + 1] for i in range(rows.shape[0])], axis=1)


def in_order(core, same, cross):
    first = jnp.where(core == 0, same, cross)
    second = jnp.where(core == 0, cross, same)
    return jnp.concatenate([first, second], axis=0)


class Chip:
    def __init__(self, p, core, same, cross, index=0):
        self.p, self.core, self.same, self.cross = p, core, same, cross
        self.index = index

    def codes(self):
        return in_order(
            self.core,
            code_block(self.p, self.same),
            code_block(self.p, self.cross),
        )

    def bring(self, targets, start, tile=None):
        p = self.p
        L = p.length
        for me in range(2):

            @pl.when(self.core == me)
            def _():
                for ref, which, first in (
                    (self.same, me, 0),
                    (self.cross, 1 - me, self.index),
                ):
                    if tile not in (None, which):
                        continue
                    to = start + (which * L if tile is None else 0)
                    for n, target in enumerate(targets):
                        for h in range(p.all):
                            at = ((first + n) * p.all + h) * L
                            target[h, to : to + L, :] = ref[at : at + L, :]


def own_chip(p, core, refs):
    pair, kv, qg = refs[:3]
    return Chip(p, core, kv, pair, 0), Chip(p, core, qg, pair, 2)


def near_chip(p, core, refs):
    return Chip(p, core, *refs[3:5])


def bring_tail(p, ref, targets, start):
    for n, target in enumerate(targets):
        for h in range(p.all):
            at = (n * p.all + h) * p.tail
            target[h, start : start + p.tail, :] = ref[at : at + p.tail, :]


def divide(core, tiles, keep, send):
    for me in range(2):

        @pl.when(core == me)
        def _():
            keep[...] = tiles[me][...]
            send[...] = tiles[1 - me][...]


class Events:
    def __init__(self, p, r, own_codes, halo_codes):
        L = p.length
        self.mine = column_of(own_codes[r * p.code_rows : (r + 1) * p.code_rows])
        self.last = halo_codes[-1:, LANES - 1 :]
        self.first_own = own_codes[0:1, 0:1]
        lo = jnp.zeros((L, 1), f32)
        for n in range(1, SESSIONS + 1):
            start = count(own_codes < n) - count(halo_codes >= n)
            lo = jnp.where(self.mine == n, start, lo)
        self.lo = lo.astype(jnp.int32)
        self.continued = count(
            jnp.logical_and(halo_codes == self.last, halo_codes > 0)
        ).astype(jnp.int32)
        self.t_pos = lax.broadcasted_iota(jnp.int32, (L, 1), 0) + r * L
        self.reads = self.mine == self.last
        self.opening = self.mine == self.first_own

    def low(self, window):
        return jnp.maximum(self.lo, self.t_pos - window + 1)


def halo_state(events, k, v, start):
    pos = lax.broadcasted_iota(jnp.int32, (k.shape[0], 1), 0) + start
    inside = jnp.broadcast_to(pos >= -events.continued, k.shape)
    phi = jnp.where(inside, feature(k.astype(f32)), 0.0).astype(bf16)
    return t_dot(phi, v)


def masked(events, score, low, start):
    L, wide = score.shape
    n_halo = -start
    s_pos = lax.broadcasted_iota(jnp.int32, (L, n_halo), 1) - n_halo
    own_pos = lax.broadcasted_iota(jnp.int32, (L, wide - n_halo), 1)
    inside = jnp.logical_and(own_pos >= low, own_pos <= events.t_pos)
    return jnp.concatenate(
        [
            jnp.where(s_pos >= low, score[:, :n_halo], MASKED),
            jnp.where(inside, score[:, n_halo:], MASKED),
        ],
        axis=1,
    )


def similar(events, score):
    own_pos = lax.broadcasted_iota(jnp.int32, score.shape, 1)
    inside = jnp.logical_and(own_pos >= events.lo, own_pos <= events.t_pos)
    return jnp.where(inside, score, 0.0).astype(bf16)


def normalized(numerator, gf):
    inverse_rms = lax.rsqrt(jnp.mean(numerator * numerator, axis=1, keepdims=True) + EPSILON)
    linear_out = numerator * inverse_rms
    grad_num = inverse_rms * (gf - linear_out * jnp.mean(gf * linear_out, axis=1, keepdims=True))
    return linear_out, grad_num.astype(bf16)


def put_stats(p, stat, h, lse, rowdot):
    for which, column in ((0, lse), (1, rowdot)):
        base = (which * p.all + h) * p.code_rows
        row = row_of(column)
        for j in range(p.code_rows):
            stat[base + j : base + j + 1, :] = row[:, j * LANES : (j + 1) * LANES]


def stat_values(p, stat):
    values = stat[...]
    used = 2 * p.all * p.code_rows
    if used < p.stat_rows:
        inside = lax.broadcasted_iota(jnp.int32, values.shape, 0) < used
        values = jnp.where(inside, values, 0.0)
    return values


def wide_column(column):
    return jnp.broadcast_to(column, (column.shape[0], LANES))


def bring_far_keys(p, core, far, targets):
    if not p.merged:
        far_at = Chip(p, core, *far)
        far_at.bring(targets, 0)
        return far_at.codes()
    bring_tail(p, far[0], targets, p.tail_fill - p.tail)
    if p.tail < p.tail_fill:
        gap = p.tail_fill - p.tail
        for target in targets:
            target[:, 0:gap, :] = jnp.zeros((p.all, gap, p.width), bf16)
    return code_block(p, far[0])


def scales(p):
    scale = 1.0 / math.sqrt(p.width)
    return scale, scale * math.log2(math.e)


def second_body(p, core_ref, win_ref, *refs):
    near, refs = refs[:5], refs[5:]
    if not p.merged:
        far, refs = refs[: p.far_refs], refs[p.far_refs :]
    if p.far:
        far_ref, refs = refs[0], refs[1:]
    out, gn_out, stats_out, state_out, ks, vs, qs, gs, stat = refs
    core = core_ref[0]
    L, C, B, D = p.length, p.chip, p.before, p.width
    scale, c2 = scales(p)
    own_keys_at, own_queries_at = own_chip(p, core, near)
    near_at = near_chip(p, core, near)
    own_keys_at.bring((ks, vs), B)
    own_queries_at.bring((qs, gs), 0, 1)
    near_at.bring((ks, vs), p.tail_fill)
    halo_codes = near_at.codes()
    begin = p.tail_fill
    if not p.merged:
        far_codes = bring_far_keys(p, core, far, (ks, vs))
        halo_codes = jnp.concatenate([far_codes, halo_codes], axis=0)
        begin = 0
    events = Events(p, 1, own_keys_at.codes(), halo_codes)

    def stream(h):
        q = qs[h]
        g = gs[h]
        gf = g.astype(f32)
        qf = q.astype(f32)
        k_part = ks[h, begin:, :]
        v_part = vs[h, begin:, :]
        v_own = vs[h, B:, :]
        score = dot_t(q, k_part)
        yield
        phi_k = feature(ks[h, B:, :].astype(f32)).astype(bf16)
        here = slice(h * D, (h + 1) * D)
        if p.far:
            start_state = far_ref[here, :]
        else:
            start_state = halo_state(events, ks[h, begin:B, :], vs[h, begin:B, :], begin - B)
            start_state = start_state.astype(bf16)
        phi_q = feature(qf).astype(bf16)
        a = dot_t(phi_q, phi_k)
        from_start = dot(phi_q, start_state)
        yield
        low = events.low(win_ref[core * p.all + h])
        score = masked(events, score, low, begin - B)
        peak = jnp.max(score, axis=1, keepdims=True) * c2
        e = jnp.exp2(score * c2 - peak)
        total = jnp.sum(e, axis=1, keepdims=True)
        yield
        inverse = 1.0 / total
        window_out = dot(e.astype(bf16), v_part) * inverse
        a = similar(events, a)
        numerator = dot(a, v_own) + jnp.where(events.reads, from_start, 0.0)
        grad_prob = dot_t(g, v_part)
        yield
        rowdot = jnp.sum(gf * window_out, axis=1, keepdims=True)
        linear_out, grad_num = normalized(numerator, gf)
        gn_out[h] = grad_num
        out[0, h] = (linear_out + window_out).astype(bf16)
        b = dot_t(grad_num, v_own)
        ds = (e * (grad_prob - rowdot)).astype(bf16)
        yield
        dq = dot(ds, k_part) * (inverse * scale)
        opening = jnp.where(events.opening, phi_q, jnp.zeros_like(phi_q))
        state_out[here, :] = t_dot(opening, grad_num)
        put_stats(p, stat, h, peak + jnp.log2(total), rowdot)
        yield
        grad_phi_q = dot(similar(events, b), phi_k) + jnp.where(
            events.reads, dot_t(grad_num, start_state), 0.0
        )
        out[1, h] = (slope(qf) * grad_phi_q + dq).astype(bf16)

    drive(stream(h) for h in range(p.all))
    stats_out[...] = stat_values(p, stat)


def start_body(p, core_ref, win_ref, *refs):
    near, refs = refs[:5], refs[5:]
    acc_out, num_out, peak_out, total_out, state_out, ks, vs, qs, gs = refs
    core = core_ref[0]
    L, C, D = p.length, p.chip, p.width
    scale, c2 = scales(p)
    own_keys_at, own_queries_at = own_chip(p, core, near)
    near_at = near_chip(p, core, near)
    own_keys_at.bring((ks, vs), C, 0)
    own_queries_at.bring((qs, gs), 0, 0)
    near_at.bring((ks, vs), 0)
    events = Events(p, 0, own_keys_at.codes(), near_at.codes())

    def stream(h):
        q = qs[h]
        score = dot_t(q, ks[h])
        yield
        phi_q = feature(q.astype(f32)).astype(bf16)
        a = dot_t(phi_q, feature(ks[h, C:, :].astype(f32)).astype(bf16))
        if not p.far:
            state_out[h * D : (h + 1) * D, :] = halo_state(
                events, ks[h, :C, :], vs[h, :C, :], -C
            )
        yield
        low = events.low(win_ref[core * p.all + h])
        score = masked(events, score, low, -C)
        peak = jnp.max(score, axis=1, keepdims=True) * c2
        e = jnp.exp2(score * c2 - peak)
        peak_out[h] = wide_column(peak)
        total_out[h] = wide_column(jnp.sum(e, axis=1, keepdims=True))
        yield
        acc_out[h] = dot(e.astype(bf16), vs[h])
        num_out[h] = dot(similar(events, a), vs[h, C:, :])

    drive(stream(h) for h in range(p.all))


def first_body(p, core_ref, win_ref, *refs):
    near, far, refs = refs[:5], refs[5 : 5 + p.far_refs], refs[5 + p.far_refs :]
    begun, refs = refs[:5], refs[5:]
    acc_in, num_in, peak_in, total_in, near_state = begun
    (second_state, second_stats), refs = refs[:2], refs[2:]
    if p.far:
        far_ref, refs = refs[0], refs[1:]
    out, gn_out, stats_out, lse_out, rowdot_out, state_out, message, ks, vs, qs, gs, stat = refs
    core = core_ref[0]
    L, B, D = p.length, p.before, p.width
    scale, c2 = scales(p)
    own_keys_at, own_queries_at = own_chip(p, core, near)
    near_at = near_chip(p, core, near)
    own_queries_at.bring((qs, gs), 0, 0)
    far_codes = bring_far_keys(p, core, far, (ks, vs))
    halo_codes = jnp.concatenate([far_codes, near_at.codes()], axis=0)
    events = Events(p, 0, own_keys_at.codes(), halo_codes)

    def stream(h):
        q = qs[h]
        gf = gs[h].astype(f32)
        here = slice(h * D, (h + 1) * D)
        score = dot_t(q, ks[h])
        if p.far:
            start_state = far_ref[here, :]
        else:
            start_state = near_state[here, :] + halo_state(events, ks[h], vs[h], -B)
            start_state = start_state.astype(bf16)
        state_out[here, :] = start_state
        yield
        phi_q = feature(q.astype(f32)).astype(bf16)
        from_start = dot(phi_q, start_state)
        low = events.low(win_ref[core * p.all + h])
        s_pos = lax.broadcasted_iota(jnp.int32, score.shape, 1) - B
        score = jnp.where(s_pos >= low, score, MASKED) * c2
        old = peak_in[h]
        peak = jnp.maximum(old[:, 0:1], jnp.max(score, axis=1, keepdims=True))
        e = jnp.exp2(score - peak)
        yield
        kept = jnp.exp2(old - peak)
        total = total_in[h] * kept + jnp.sum(e, axis=1, keepdims=True)
        window_out = (acc_in[h] * kept + dot(e.astype(bf16), vs[h])) / total
        numerator = num_in[h] + jnp.where(events.reads, from_start, 0.0)
        linear_out, grad_num = normalized(numerator, gf)
        gn_out[h] = grad_num
        yield
        rowdot = jnp.sum(gf * window_out, axis=1, keepdims=True)
        out[h] = (linear_out + window_out).astype(bf16)
        opening = jnp.where(events.opening, phi_q, jnp.zeros_like(phi_q))
        message[here, :] = (second_state[here, :] + t_dot(opening, grad_num)).astype(bf16)
        lse = (peak + jnp.log2(total))[:, 0:1]
        lse_out[h] = wide_column(lse)
        rowdot_out[h] = wide_column(rowdot)
        yield
        put_stats(p, stat, h, lse, rowdot)

    drive(stream(h) for h in range(p.all))
    values = stat_values(p, stat)
    stats_out[...] = values
    for tile, values in enumerate((values, second_stats[...])):
        for n in range(3):
            piece = values.astype(bf16)
            at = p.state_rows + (3 * tile + n) * p.stat_rows
            message[at : at + p.stat_rows, :] = piece
            values = values - piece.astype(f32)


def grad_body(p, core_ref, win_ref, *refs):
    near, far, refs = refs[:5], refs[5 : 5 + p.far_refs], refs[5 + p.far_refs :]
    (first_out, gn, lse_in, rowdot_in, state_in, second), refs = refs[:6], refs[6:]
    keep, send, ks, vs, qs, gs, out = refs
    core = core_ref[0]
    L, B, D = p.length, p.before, p.width
    scale, c2 = scales(p)
    own_keys_at, own_queries_at = own_chip(p, core, near)
    near_at = near_chip(p, core, near)
    own_keys_at.bring((ks, vs), B, 0)
    own_queries_at.bring((qs, gs), 0, 0)
    near_at.bring((ks, vs), p.tail_fill)
    far_codes = bring_far_keys(p, core, far, (ks, vs))
    halo_codes = jnp.concatenate([far_codes, near_at.codes()], axis=0)
    events = Events(p, 0, own_keys_at.codes(), halo_codes)

    def stream(h):
        q = qs[h]
        score = dot_t(q, ks[h])
        grad_prob = dot_t(gs[h], vs[h])
        yield
        grad_num = gn[h]
        b = dot_t(grad_num, vs[h, B:, :])
        from_start = dot_t(grad_num, state_in[h * D : (h + 1) * D, :])
        yield
        low = events.low(win_ref[core * p.all + h])
        score = masked(events, score, low, -B)
        prob = jnp.exp2(score * c2 - lse_in[h][:, 0:1])
        ds = (prob * (grad_prob - rowdot_in[h][:, 0:1])).astype(bf16)
        yield
        dq = dot(ds, ks[h]) * scale
        phi_k = feature(ks[h, B:, :].astype(f32)).astype(bf16)
        grad_phi_q = dot(similar(events, b), phi_k) + jnp.where(events.reads, from_start, 0.0)
        yield
        out[0, h] = first_out[h]
        out[1, h] = (slope(q.astype(f32)) * grad_phi_q + dq).astype(bf16)

    drive(stream(h) for h in range(p.all))
    divide(core, (out, second), keep, send)


def query_side(p, core, windows, near, far, far_state, near_queries, far_queries):
    vmem = pl.BlockSpec(memory_space=pltpu.VMEM)
    smem = pl.BlockSpec(memory_space=pltpu.SMEM)

    def kernel(body, micros, args, outs, scratch):
        return pl.pallas_call(
            functools.partial(body, p),
            out_shape=[jax.ShapeDtypeStruct(shape, kind) for shape, kind in outs],
            in_specs=[smem, smem] + [vmem] * len(args),
            out_specs=[vmem] * len(outs),
            scratch_shapes=[pltpu.VMEM(shape, kind) for shape, kind in scratch],
            **params(micros),
            name=body.__name__,
        )(core, windows, *args)

    tile = (p.all, p.length, p.width)
    both = (2, *tile)
    stats = ((p.stat_rows, p.width), f32)
    state = (p.state_rows, p.width)
    rows = [(tile, bf16)] * 2
    far_state = [far_state] if p.far else []

    def keys(n):
        return [((p.all, n, p.width), bf16)] * 2

    second, grad_1, stats_1, state_1 = kernel(
        second_body,
        5.7,
        [*near, *(() if p.merged else far), *far_state],
        [(both, bf16), (tile, bf16), stats, (state, f32)],
        keys(p.before + p.chip) + rows + [stats],
    )
    begun = kernel(
        start_body,
        3.0,
        near,
        [(tile, f32)] * 2 + [((p.all, p.length, LANES), f32)] * 2 + [(state, f32)],
        keys(p.chip + p.length) + rows,
    )
    state_1, *_ = lax.optimization_barrier((state_1, *near_queries))
    first, grad_0, stats_0, lse, rowdot, start_state, message = kernel(
        first_body,
        2.0,
        [*near, *far, *begun, state_1, stats_1, *far_state],
        [(tile, bf16)] * 2
        + [stats]
        + [((p.all, p.length, LANES), f32)] * 2
        + [(state, bf16), ((p.state_rows + 6 * p.stat_rows, p.width), bf16)],
        keys(p.tail_fill) + rows + [stats],
    )

    def finish():
        return kernel(
            grad_body,
            3.5,
            [*near, *far, first, grad_0, lse, rowdot, start_state, second],
            [(both, bf16)] * 2,
            keys(p.before + p.length) + rows + [(both, bf16)],
        )

    return grad_1, stats_1, grad_0, stats_0, message, finish


def stats_of(p, values, head):
    result = []
    for which in range(2):
        base = (which * p.all + head) * p.code_rows
        result.append(flat(values[base : base + p.code_rows]))
    return result


def unpack_stats(p, message, tile):
    total = jnp.zeros((p.stat_rows, LANES), f32)
    for n in reversed(range(3)):
        at = p.state_rows + (3 * tile + n) * p.stat_rows
        total = total + message[at : at + p.stat_rows, :].astype(f32)
    return total


def own_body(p, r, core_ref, win_ref, *refs):
    near, (gn, stats_in), refs = refs[:3], refs[3:5], refs[5:]
    if r == 0:
        (dk_i, dv_i), refs = refs[:2], refs[2:]
    dk_o, dv_o, ks, vs, qs, gs = refs
    core = core_ref[0]
    L, C, D = p.length, p.chip, p.width
    scale = 1.0 / math.sqrt(D)
    c2 = scale * math.log2(math.e)
    own_keys_at, own_queries_at = own_chip(p, core, near)
    own_keys_at.bring((ks, vs), 0)
    own_queries_at.bring((qs, gs), 0, r)
    own_codes = own_keys_at.codes()
    code = column_of(own_codes)
    hi_all = jnp.zeros((C, 1), f32)
    for n in range(1, SESSIONS + 1):
        hi_all = jnp.where(code == n, count(own_codes <= n) - 1.0, hi_all)
    hi_all = hi_all.astype(jnp.int32)
    stats = stats_in[...]

    def stream(h, tile):
        window = win_ref[core * p.all + h]
        lse, rowdot = stats_of(p, stats, h)
        rows = slice(tile * L, (tile + 1) * L)
        k, v = ks[h, rows, :], vs[h, rows, :]
        q, g = qs[h], gs[h]
        score = dot_t(k, q)
        grad_prob = dot_t(v, g)
        yield
        phi_q = feature(q.astype(f32)).astype(bf16)
        kf = k.astype(f32)
        grad_num = gn[h]
        a = dot_t(feature(kf).astype(bf16), phi_q)
        b = dot_t(v, grad_num)
        yield
        hi = hi_all[rows]
        s_pos = lax.broadcasted_iota(jnp.int32, (L, 1), 0) + tile * L
        t_pos = lax.broadcasted_iota(jnp.int32, (L, L), 1) + r * L
        alike = t_pos <= hi
        if tile == r:
            alike = jnp.logical_and(alike, t_pos >= s_pos)
        allowed = jnp.logical_and(alike, t_pos < s_pos + window)
        prob = jnp.exp2(jnp.where(allowed, score * c2 - lse, MASKED))
        ds = (prob * (grad_prob - rowdot)).astype(bf16)
        yield
        dk = dot(ds, q) * scale
        dv = dot(prob.astype(bf16), g)
        a = jnp.where(alike, a, 0.0).astype(bf16)
        b = jnp.where(alike, b, 0.0).astype(bf16)
        yield
        dk = dk + slope(kf) * dot(b, phi_q)
        dv = dv + dot(a, grad_num)
        if r == 0:
            dk_o[h] = dk_i[h, rows, :] + dk
            dv_o[h] = dv_i[h, rows, :] + dv
        else:
            dk_o[h, rows, :] = dk
            dv_o[h, rows, :] = dv

    drive(stream(h, tile) for h in range(p.all) for tile in range(r + 1))


def own_keys(p, r, core, windows, near, gn, stats, carried=()):
    vmem = pl.BlockSpec(memory_space=pltpu.VMEM)
    smem = pl.BlockSpec(memory_space=pltpu.SMEM)
    full = jax.ShapeDtypeStruct((p.all, p.chip if r else p.length, p.width), f32)
    args = [*near[:3], gn, stats, *carried]
    keys = pltpu.VMEM((p.all, p.chip, p.width), bf16)
    tile = pltpu.VMEM((p.all, p.length, p.width), bf16)
    return pl.pallas_call(
        functools.partial(own_body, p, r),
        out_shape=[full, full],
        in_specs=[smem, smem] + [vmem] * len(args),
        out_specs=[vmem] * 2,
        scratch_shapes=[keys, keys, tile, tile],
        **params(4.0 if r else 2.0),
        name="own_keys",
    )(core, windows, *args)


def later_body(p, core_ref, win_ref, *refs):
    near, refs = refs[:5], refs[5:]
    far, refs = refs[: p.far_refs], refs[p.far_refs :]
    (message_1, message_2), sums, refs = refs[:2], (refs[2:4], refs[4:6]), refs[6:]
    if p.far:
        far_ref, refs = refs[0], refs[1:]
    keep, send, ks, vs, qs, gs, first, second = refs
    core = core_ref[0]
    L, C, D = p.length, p.chip, p.width
    N = p.tail_fill
    scale = 1.0 / math.sqrt(D)
    c2 = scale * math.log2(math.e)
    own_keys_at, _ = own_chip(p, core, near)
    near_at = near_chip(p, core, near)
    own_keys_at.bring((ks, vs), 0)
    near_at.bring((qs, gs), 0)
    own_codes = own_keys_at.codes()
    near_codes = near_at.codes()
    if p.merged:
        far_codes = code_block(p, far[0])
        bring_tail(p, far[0], (qs, gs), C)
        if p.tail < p.tail_fill:
            gap = p.tail_fill - p.tail
            qs[:, C + p.tail :, :] = jnp.zeros((p.all, gap, D), bf16)
            gs[:, C + p.tail :, :] = jnp.zeros((p.all, gap, D), bf16)
    else:
        far_at = Chip(p, core, *far)
        far_at.bring((qs, gs), C)
        far_codes = far_at.codes()
    after_codes = jnp.concatenate([near_codes, far_codes], axis=0)
    code = column_of(own_codes)
    final = own_codes[2 * p.code_rows - 1 :, LANES - 1 :]
    hi_last = C - 1 + count(after_codes == final)
    hi = jnp.where(code == final, hi_last, -1.0).astype(jnp.int32)
    first_next = near_codes[0:1, 0:1]
    goes_on = jnp.logical_and(first_next > 0, first_next == far_codes[0:1, 0:1])
    tiles = [unpack_stats(p, message_1, 0), unpack_stats(p, message_1, 1)]
    tiles += [unpack_stats(p, message_2, n) for n in range(N // L)]

    def stream(h, r):
        far_here = r == 1 or not p.merged
        wide = C + N if far_here else C
        rows = slice(r * L, (r + 1) * L)
        uses = code[rows] == first_next
        dk_i, dv_i = sums[r]
        window = win_ref[core * p.all + h]
        lse, rowdot = (
            jnp.concatenate(x, axis=1) for x in zip(*(stats_of(p, tile, h) for tile in tiles[: wide // L]))
        )
        k, v = ks[h, rows, :], vs[h, rows, :]
        q, g = qs[h, 0:wide, :], gs[h, 0:wide, :]
        score = dot_t(k, q)
        grad_prob = dot_t(v, g)
        yield
        here = slice(h * D, (h + 1) * D)
        if p.far:
            later_state = far_ref[here, :]
        else:
            later_state = message_1[here, :]
            if far_here:
                later_state = (
                    later_state.astype(f32)
                    + jnp.where(goes_on, message_2[here, :].astype(f32), 0.0)
                ).astype(bf16)
        kf = k.astype(f32)
        phi_k = feature(kf).astype(bf16)
        dk_lin = dot_t(v, later_state)
        dv_lin = dot(phi_k, later_state)
        yield
        s_pos = lax.broadcasted_iota(jnp.int32, (L, 1), 0) + r * L
        t_pos = lax.broadcasted_iota(jnp.int32, (L, wide), 1) + C
        allowed = t_pos <= jnp.minimum(hi[rows], s_pos + window - 1)
        prob = jnp.exp2(jnp.where(allowed, score * c2 - lse, MASKED))
        ds = (prob * (grad_prob - rowdot)).astype(bf16)
        yield
        dk = dot(ds, q) * scale
        dv = dot(prob.astype(bf16), g)
        yield
        out = (first, second)[r]
        dk = dk_i[h, rows, :] + dk + slope(kf) * jnp.where(uses, dk_lin, 0.0)
        dv = dv_i[h, rows, :] + dv + jnp.where(uses, dv_lin, 0.0)
        out[0, h] = dk.astype(bf16)
        out[1, h] = dv.astype(bf16)

    drive(stream(h, r) for h in range(p.all) for r in range(2))
    divide(core, (first, second), keep, send)


def later_keys(p, core, windows, near, far, messages, sums, far_state):
    vmem = pl.BlockSpec(memory_space=pltpu.VMEM)
    smem = pl.BlockSpec(memory_space=pltpu.SMEM)
    args = [*near, *far, *messages, *sums] + ([far_state] if p.far else [])
    both = jax.ShapeDtypeStruct((2, p.all, p.length, p.width), bf16)
    keys = pltpu.VMEM((p.all, p.chip, p.width), bf16)
    tall = pltpu.VMEM((p.all, p.chip + p.tail_fill, p.width), bf16)
    return pl.pallas_call(
        functools.partial(later_body, p),
        out_shape=[both, both],
        in_specs=[smem, smem] + [vmem] * len(args),
        out_specs=[vmem, vmem],
        scratch_shapes=[keys, keys, tall, tall] + [pltpu.VMEM(both.shape, bf16)] * 2,
        **params(5.5),
        name="later_keys",
    )(core, windows, *args)


def unpack_body(p, core_ref, mine, theirs, out_a, out_b, scratch):
    core = core_ref[0]
    for n in range(2):
        for h in range(p.all):
            scratch[n, core * p.all + h] = mine[n, h].astype(f32)
            scratch[n, (1 - core) * p.all + h] = theirs[n, h].astype(f32)
    for n, out in ((0, out_a), (1, out_b)):
        out[...] = jnp.swapaxes(scratch[n], 0, 1).astype(bf16)


def unpack(p, core, mine, theirs):
    vmem = pl.BlockSpec(memory_space=pltpu.VMEM)
    out = jax.ShapeDtypeStruct((p.length, p.heads, p.width), bf16)
    return pl.pallas_call(
        functools.partial(unpack_body, p),
        out_shape=[out, out],
        in_specs=[pl.BlockSpec(memory_space=pltpu.SMEM)] + [vmem] * 2,
        out_specs=[vmem, vmem],
        scratch_shapes=[pltpu.VMEM((2, p.heads, p.length, p.width), f32)],
        **params(1.4),
        name="unpack",
    )(core, mine, theirs)


def folded(session, state, backward):
    sessions = lax.all_gather(session, "ctx")
    states = lax.all_gather(state, "ctx")
    count = lax.axis_size("ctx")
    here = lax.axis_index("ctx")

    def one(hop, carry):
        held, total = carry
        source = count - 1 - hop if backward else hop
        new = lax.dynamic_index_in_dim(sessions, source, 0, False)
        first, last = new[0], new[1]
        part = lax.dynamic_index_in_dim(states, source, 0, False).astype(f32)
        entering, leaving = (last, first) if backward else (first, last)
        whole = jnp.logical_and(entering == held, entering == leaving)
        return leaving, part + jnp.where(whole, total, 0.0)

    steps = count - 1 - here if backward else here
    start = (jnp.zeros((), jnp.int32) - 1, jnp.zeros(state.shape, f32))
    return lax.fori_loop(0, steps, one, start)[1].astype(bf16)


def shards(p, queries, key_vectors, value_vectors, targets, token_weights, sessions, window_size):
    L = p.length
    chips = lax.axis_size("ctx")
    core_id = lax.axis_index("pair").astype(jnp.int32)
    core = core_id.reshape(1)
    def move(x, target):
        pairs = []
        for c in range(chips):
            for i in range(2):
                to, j = target(c, i)
                if 0 <= to < chips:
                    pairs.append((2 * c + i, 2 * to + j))
        return lax.ppermute(x, AXES, pairs)

    packed = pack(
        p,
        core,
        queries,
        key_vectors,
        value_vectors,
        targets,
        token_weights.reshape(-1, LANES),
        sessions.reshape(-1, LANES),
    )
    for_pair, payloads = packed[0], packed[1:]

    def exchange(same, cross, by):
        return (
            move(same, lambda c, i: (c + by, i)),
            move(cross, lambda c, i: (c + by, 1 - i)),
        )

    pair = move(for_pair, lambda c, i: (c, 1 - i))
    kv_same, kv_cross, qg_same, qg_cross = payloads
    near_keys = exchange(kv_same, kv_cross, 1)
    near_queries = exchange(qg_same, qg_cross, -1)
    if p.merged:
        last_keys, first_queries = make_tails(p, core, pair, kv_same, qg_same)
        last_keys, key_part = lax.optimization_barrier((last_keys, near_keys[0]))
        near_keys = (key_part, near_keys[1])
        first_queries, query_part = lax.optimization_barrier((first_queries, near_queries[0]))
        near_queries = (query_part, near_queries[1])
        far_keys = (move(last_keys, lambda c, i: (c + 2, i)),)
        far_queries = (move(first_queries, lambda c, i: (c - 2, i)),)
    else:
        far_keys = exchange(kv_same, kv_cross, 2)
        far_queries = exchange(qg_same, qg_cross, -2)
    own = (pair, kv_same, qg_same)
    near = (*own, *near_keys)

    far_before = far_after = None
    if p.far:
        both = lax.all_gather(sessions, "pair")
        chip_ends = jnp.stack([both[0, 0], both[1, -1]])

        total = jnp.zeros((p.all, p.width, p.width), f32)
        keys_here = kv_same[: p.rows - EXTRA]
        keys_here = keys_here.reshape(2, p.all, L, p.width)
        keys_pair = pair[: p.pair_rows - EXTRA].reshape(4, p.all, L, p.width)[:2]
        for part, owner in ((keys_here, core_id), (keys_pair, 1 - core_id)):
            rows = lax.dynamic_index_in_dim(both, owner, 0, False)
            phi = feature(part[0].astype(f32))
            phi = jnp.where((rows == chip_ends[1])[None, :, None], phi, 0.0).astype(bf16)
            total = total + jnp.einsum(
                "hsk,hsd->hkd", phi, part[1], preferred_element_type=f32
            )
        far_before = folded(chip_ends, total.astype(bf16), False).reshape(-1, p.width)

    grad_1, stats_1, grad_0, stats_0, message, finish = query_side(
        p, core, window_size, near, far_keys, far_before, near_queries, far_queries
    )
    message, grad_1 = lax.optimization_barrier((message, grad_1))
    sums_1 = own_keys(p, 1, core, window_size, near, grad_1, stats_1)
    messages = (
        move(message, lambda c, i: (c - 1, i)),
        move(message, lambda c, i: (c - 2, i)),
    )
    if p.far:
        state = message[: p.state_rows].reshape(p.all, p.width, p.width)
        far_after = folded(chip_ends, state, True).reshape(-1, p.width)
    keep_q, send_q = finish()
    sums_0 = own_keys(p, 0, core, window_size, near, grad_0, stats_0, sums_1)
    keep_k, send_k = later_keys(
        p, core, window_size, (*own, *near_queries), far_queries, messages, (*sums_0, *sums_1), far_after
    )
    attended, grad_queries = unpack(p, core, keep_q, move(send_q, lambda c, i: (c, 1 - i)))
    grad_keys, grad_values = unpack(p, core, keep_k, move(send_k, lambda c, i: (c, 1 - i)))
    return (attended, grad_queries, grad_keys, grad_values)


def solution(mesh):
    rows = P(("groups", "ctx", "pair"), "head", None)
    events = P(("groups", "ctx", "pair"))

    def run(queries, key_vectors, value_vectors, targets, token_weights, sessions, window_size):
        total = queries.shape[0] // mesh.shape["groups"]
        length = total // (mesh.shape["ctx"] * mesh.shape["pair"])
        heads = queries.shape[1] // mesh.shape["head"]
        p = Plan(length, heads, queries.shape[2], total)
        return jax.shard_map(
            functools.partial(shards, p),
            mesh=mesh,
            in_specs=(rows, rows, rows, rows, events, events, P("head")),
            out_specs=(rows, rows, rows, rows),
            check_vma=False,
        )(queries, key_vectors, value_vectors, targets, token_weights, sessions, window_size)

    return run
```

```python
import functools
import math

import jax
import jax.numpy as jnp
from jax import lax
from jax.experimental import pallas as pl
from jax.experimental.pallas import tpu as pltpu
from jax.sharding import PartitionSpec as P

WIN = 1024
SESSIONS = 6
EPSILON = 1e-06
MASKED = -1e30
AXES = ("ctx", "pair")
EXTRA = 16
LANES = 128
VMEM_LIMIT = 28 << 20

f32 = jnp.float32
bf16 = jnp.bfloat16


def dot(a, b):
    return lax.dot_general(a, b, (((1,), (0,)), ((), ())), preferred_element_type=f32)


def dot_t(a, b):
    return lax.dot_general(a, b, (((1,), (1,)), ((), ())), preferred_element_type=f32)


def t_dot(a, b):
    return lax.dot_general(a, b, (((0,), (0,)), ((), ())), preferred_element_type=f32)


def feature(x):
    return jnp.where(x > 0, x + 1.0, jnp.exp(jnp.minimum(x, 0.0)))


def slope(x):
    return jnp.where(x > 0, 1.0, jnp.exp(jnp.minimum(x, 0.0)))


def params(micros):
    return dict(
        compiler_params=pltpu.CompilerParams(vmem_limit_bytes=VMEM_LIMIT),
        cost_estimate=pl.CostEstimate(
            flops=int(micros * 1.15e9), bytes_accessed=int(micros * 1e6), transcendentals=0
        ),
    )


def row_of(column):
    n = column.shape[0]
    return jnp.concatenate(
        [
            jnp.transpose(jnp.broadcast_to(column[i : i + LANES], (LANES, LANES)))[0:1]
            for i in range(0, n, LANES)
        ],
        axis=1,
    )


def column_of(rows):
    return jnp.concatenate(
        [
            jnp.transpose(jnp.broadcast_to(rows[i : i + 1], (LANES, LANES)))[:, 0:1]
            for i in range(rows.shape[0])
        ],
        axis=0,
    )


class Plan:
    def __init__(self, length, heads, width, total):
        self.length = length
        self.heads = heads
        self.all = heads // 2
        self.width = width
        self.chip = 2 * length
        longest = total // 3
        reach = min(WIN, longest) - 1
        tail = max(reach - self.chip, 0)
        self.far = longest - 1 > 2 * self.chip or longest - 1 > reach
        self.merged = tail <= length
        self.tail = -(-tail // 16) * 16 if self.merged else length
        self.tail_fill = length if self.merged else self.chip
        self.before = self.tail_fill + self.chip
        self.code_rows = length // LANES
        self.rows = self.all * 2 * length + EXTRA
        self.tail_rows = self.all * 2 * self.tail + EXTRA
        self.pair_rows = self.all * 4 * length + EXTRA
        self.stat_rows = -(-2 * self.all * self.code_rows // 16) * 16
        self.state_rows = self.all * width
        self.far_refs = 1 if self.merged else 2


def pack_body(p, core_ref, q_ref, k_ref, v_ref, t_ref, w_ref, s_ref, *rest):
    number = (len(rest) - 3) // 2
    outs, staged = rest[:number], rest[number : 2 * number]
    landed, sems, out_sems = rest[2 * number :]
    L = p.length
    copies = [
        pltpu.make_async_copy(ref, landed.at[n], sems.at[n])
        for n, ref in enumerate((k_ref, v_ref, q_ref, t_ref))
    ]
    for copy_in in copies:
        copy_in.start()
    weight = column_of(w_ref[...].astype(f32))
    codes = jnp.concatenate(
        [s_ref[...].astype(f32) + 1.0, jnp.zeros((EXTRA - p.code_rows, LANES), f32)], axis=0
    ).astype(bf16)
    for ref in staged:
        ref[ref.shape[0] - EXTRA :, :] = codes

    def pack_for(me):
        leaving = []

        def leave(x, part, parts, rows):
            here = slice(part * rows, (part + 1) * rows + EXTRA * (part == parts - 1))
            copy_out = pltpu.make_async_copy(
                staged[x].at[here, :], outs[x].at[here, :], out_sems.at[len(leaving)]
            )
            copy_out.start()
            leaving.append(copy_out)

        for n in range(4):
            copies[n].wait()
            x = jnp.swapaxes(landed[n].astype(f32), 0, 1)
            if n == 3:
                x = x * weight[None]
            x = x.astype(bf16)
            mine = x[me * p.all : (me + 1) * p.all]
            other = x[(1 - me) * p.all : (2 - me) * p.all]
            to = n % 2 * p.all
            for at, heads in ((1 + n // 2 * 2, mine), (2 + n // 2 * 2, other)):
                for h in range(p.all):
                    staged[at][(to + h) * L : (to + h + 1) * L, :] = heads[h]
                leave(at, n % 2, 2, p.all * L)
            for h in range(p.all):
                staged[0][(n * p.all + h) * L : (n * p.all + h + 1) * L, :] = other[h]
            leave(0, n, 4, p.all * L)
        for copy_out in leaving:
            copy_out.wait()

    for me in range(2):

        @pl.when(core_ref[0] == me)
        def _():
            pack_for(me)


def pack(p, core, q, k, v, targets, weights, sessions):
    rows = [p.pair_rows] + [p.rows] * 4
    shapes = [(n, p.width) for n in rows]
    vmem = pl.BlockSpec(memory_space=pltpu.VMEM)
    hbm = pl.BlockSpec(memory_space=pl.ANY)
    return pl.pallas_call(
        functools.partial(pack_body, p),
        out_shape=[jax.ShapeDtypeStruct(x, bf16) for x in shapes],
        in_specs=[pl.BlockSpec(memory_space=pltpu.SMEM)] + [hbm] * 4 + [vmem] * 2,
        out_specs=[hbm] * len(shapes),
        scratch_shapes=[pltpu.VMEM(x, bf16) for x in shapes]
        + [
            pltpu.VMEM((4, p.length, p.heads, p.width), bf16),
            pltpu.SemaphoreType.DMA((4,)),
            pltpu.SemaphoreType.DMA((12,)),
        ],
        compiler_params=pltpu.CompilerParams(vmem_limit_bytes=56 << 20),
        name="pack",
    )(core, q, k, v, targets, weights, sessions)


def tails_body(p, core_ref, pair, own_keys, own_queries, keys, queries):
    L = p.length

    def tails_for(me):
        sources = [(pair, 0), (own_queries, 0)] if me == 0 else [(own_keys, 0), (pair, 2)]
        for out, (ref, first), lead in zip((keys, queries), sources, (L - p.tail, 0)):
            for n in range(2 * p.all):
                at = (first * p.all + n) * L + lead
                out[n * p.tail : (n + 1) * p.tail, :] = ref[at : at + p.tail, :]
            out[p.tail_rows - EXTRA :, :] = ref[ref.shape[0] - EXTRA :, :]

    for me in range(2):

        @pl.when(core_ref[0] == me)
        def _():
            tails_for(me)


def make_tails(p, core, pair, own_keys, own_queries):
    vmem = pl.BlockSpec(memory_space=pltpu.VMEM)
    out = jax.ShapeDtypeStruct((p.tail_rows, p.width), bf16)
    return pl.pallas_call(
        functools.partial(tails_body, p),
        out_shape=[out, out],
        in_specs=[pl.BlockSpec(memory_space=pltpu.SMEM), vmem, vmem, vmem],
        out_specs=[vmem, vmem],
        **params(1.0),
        name="tails",
    )(core, pair, own_keys, own_queries)


def code_block(p, ref):
    return ref[ref.shape[0] - EXTRA :, :].astype(f32)[: p.code_rows]


def count(condition):
    return jnp.sum(
        jnp.sum(jnp.where(condition, 1.0, 0.0), axis=1, keepdims=True), axis=0, keepdims=True
    )


def drive(streams):
    streams = list(streams)
    while streams:
        streams = [x for x in streams if next(x, streams) is not streams]


def flat(rows):
    return jnp.concatenate([rows[i : i + 1] for i in range(rows.shape[0])], axis=1)


def in_order(core, same, cross):
    first = jnp.where(core == 0, same, cross)
    second = jnp.where(core == 0, cross, same)
    return jnp.concatenate([first, second], axis=0)


class Chip:
    def __init__(self, p, core, same, cross, index=0):
        self.p, self.core, self.same, self.cross = p, core, same, cross
        self.index = index

    def codes(self):
        return in_order(
            self.core,
            code_block(self.p, self.same),
            code_block(self.p, self.cross),
        )

    def bring(self, targets, start, tile=None):
        p = self.p
        L = p.length
        for me in range(2):

            @pl.when(self.core == me)
            def _():
                for ref, which, first in (
                    (self.same, me, 0),
                    (self.cross, 1 - me, self.index),
                ):
                    if tile not in (None, which):
                        continue
                    to = start + (which * L if tile is None else 0)
                    for n, target in enumerate(targets):
                        for h in range(p.all):
                            at = ((first + n) * p.all + h) * L
                            target[h, to : to + L, :] = ref[at : at + L, :]


def own_chip(p, core, refs):
    pair, kv, qg = refs[:3]
    return Chip(p, core, kv, pair, 0), Chip(p, core, qg, pair, 2)


def near_chip(p, core, refs):
    return Chip(p, core, *refs[3:5])


def bring_tail(p, ref, targets, start):
    for n, target in enumerate(targets):
        for h in range(p.all):
            at = (n * p.all + h) * p.tail
            target[h, start : start + p.tail, :] = ref[at : at + p.tail, :]


def divide(core, tiles, keep, send):
    for me in range(2):

        @pl.when(core == me)
        def _():
            keep[...] = tiles[me][...]
            send[...] = tiles[1 - me][...]


class Events:
    def __init__(self, p, r, own_codes, halo_codes):
        L = p.length
        self.mine = column_of(own_codes[r * p.code_rows : (r + 1) * p.code_rows])
        self.last = halo_codes[-1:, LANES - 1 :]
        self.first_own = own_codes[0:1, 0:1]
        lo = jnp.zeros((L, 1), f32)
        for n in range(1, SESSIONS + 1):
            start = count(own_codes < n) - count(halo_codes >= n)
            lo = jnp.where(self.mine == n, start, lo)
        self.lo = lo.astype(jnp.int32)
        self.continued = count(
            jnp.logical_and(halo_codes == self.last, halo_codes > 0)
        ).astype(jnp.int32)
        self.t_pos = lax.broadcasted_iota(jnp.int32, (L, 1), 0) + r * L
        self.reads = self.mine == self.last
        self.opening = self.mine == self.first_own

    def low(self, window):
        return jnp.maximum(self.lo, self.t_pos - window + 1)


def halo_state(events, k, v, start):
    pos = lax.broadcasted_iota(jnp.int32, (k.shape[0], 1), 0) + start
    inside = jnp.broadcast_to(pos >= -events.continued, k.shape)
    phi = jnp.where(inside, feature(k.astype(f32)), 0.0).astype(bf16)
    return t_dot(phi, v)


def masked(events, score, low, start):
    L, wide = score.shape
    n_halo = -start
    s_pos = lax.broadcasted_iota(jnp.int32, (L, n_halo), 1) - n_halo
    own_pos = lax.broadcasted_iota(jnp.int32, (L, wide - n_halo), 1)
    inside = jnp.logical_and(own_pos >= low, own_pos <= events.t_pos)
    return jnp.concatenate(
        [
            jnp.where(s_pos >= low, score[:, :n_halo], MASKED),
            jnp.where(inside, score[:, n_halo:], MASKED),
        ],
        axis=1,
    )


def similar(events, score):
    own_pos = lax.broadcasted_iota(jnp.int32, score.shape, 1)
    inside = jnp.logical_and(own_pos >= events.lo, own_pos <= events.t_pos)
    return jnp.where(inside, score, 0.0).astype(bf16)


def normalized(numerator, gf):
    inverse_rms = lax.rsqrt(jnp.mean(numerator * numerator, axis=1, keepdims=True) + EPSILON)
    linear_out = numerator * inverse_rms
    grad_num = inverse_rms * (gf - linear_out * jnp.mean(gf * linear_out, axis=1, keepdims=True))
    return linear_out, grad_num.astype(bf16)


def put_stats(p, stat, h, lse, rowdot):
    for which, column in ((0, lse), (1, rowdot)):
        base = (which * p.all + h) * p.code_rows
        row = row_of(column)
        for j in range(p.code_rows):
            stat[base + j : base + j + 1, :] = row[:, j * LANES : (j + 1) * LANES]


def stat_values(p, stat):
    values = stat[...]
    used = 2 * p.all * p.code_rows
    if used < p.stat_rows:
        inside = lax.broadcasted_iota(jnp.int32, values.shape, 0) < used
        values = jnp.where(inside, values, 0.0)
    return values


def wide_column(column):
    return jnp.broadcast_to(column, (column.shape[0], LANES))


def bring_far_keys(p, core, far, targets):
    if not p.merged:
        far_at = Chip(p, core, *far)
        far_at.bring(targets, 0)
        return far_at.codes()
    bring_tail(p, far[0], targets, p.tail_fill - p.tail)
    if p.tail < p.tail_fill:
        gap = p.tail_fill - p.tail
        for target in targets:
            target[:, 0:gap, :] = jnp.zeros((p.all, gap, p.width), bf16)
    return code_block(p, far[0])


def scales(p):
    scale = 1.0 / math.sqrt(p.width)
    return scale, scale * math.log2(math.e)


def second_body(p, core_ref, win_ref, *refs):
    near, refs = refs[:5], refs[5:]
    if not p.merged:
        far, refs = refs[: p.far_refs], refs[p.far_refs :]
    if p.far:
        far_ref, refs = refs[0], refs[1:]
    (out, gn_out, stats_out, state_out), refs = refs[:4], refs[4:]
    acc_out, num_out, peak_out, total_out, near_out, ks, vs, qs, gs, stat = refs
    core = core_ref[0]
    L, C, B, D = p.length, p.chip, p.before, p.width
    scale, c2 = scales(p)
    own_keys_at, own_queries_at = own_chip(p, core, near)
    near_at = near_chip(p, core, near)
    own_keys_at.bring((ks, vs), B)
    own_queries_at.bring((qs, gs), 0)
    near_at.bring((ks, vs), p.tail_fill)
    own_codes = own_keys_at.codes()
    halo_codes = near_at.codes()
    events_0 = Events(p, 0, own_codes, halo_codes)
    begin = p.tail_fill
    if not p.merged:
        far_codes = bring_far_keys(p, core, far, (ks, vs))
        halo_codes = jnp.concatenate([far_codes, halo_codes], axis=0)
        begin = 0
    events = Events(p, 1, own_codes, halo_codes)

    def stream(h):
        q = qs[h, L:, :]
        g = gs[h, L:, :]
        gf = g.astype(f32)
        qf = q.astype(f32)
        k_part = ks[h, begin:, :]
        v_part = vs[h, begin:, :]
        v_own = vs[h, B:, :]
        score = dot_t(q, k_part)
        yield
        phi_k = feature(ks[h, B:, :].astype(f32)).astype(bf16)
        here = slice(h * D, (h + 1) * D)
        if p.far:
            start_state = far_ref[here, :]
        else:
            start_state = halo_state(events, ks[h, begin:B, :], vs[h, begin:B, :], begin - B)
            start_state = start_state.astype(bf16)
        phi_q = feature(qf).astype(bf16)
        a = dot_t(phi_q, phi_k)
        from_start = dot(phi_q, start_state)
        yield
        low = events.low(win_ref[core * p.all + h])
        score = masked(events, score, low, begin - B)
        peak = jnp.max(score, axis=1, keepdims=True) * c2
        e = jnp.exp2(score * c2 - peak)
        total = jnp.sum(e, axis=1, keepdims=True)
        yield
        inverse = 1.0 / total
        window_out = dot(e.astype(bf16), v_part) * inverse
        a = similar(events, a)
        numerator = dot(a, v_own) + jnp.where(events.reads, from_start, 0.0)
        grad_prob = dot_t(g, v_part)
        yield
        rowdot = jnp.sum(gf * window_out, axis=1, keepdims=True)
        linear_out, grad_num = normalized(numerator, gf)
        gn_out[h] = grad_num
        out[0, h] = (linear_out + window_out).astype(bf16)
        b = dot_t(grad_num, v_own)
        ds = (e * (grad_prob - rowdot)).astype(bf16)
        yield
        dq = dot(ds, k_part) * (inverse * scale)
        opening = jnp.where(events.opening, phi_q, jnp.zeros_like(phi_q))
        state_out[here, :] = t_dot(opening, grad_num)
        put_stats(p, stat, h, peak + jnp.log2(total), rowdot)
        yield
        grad_phi_q = dot(similar(events, b), phi_k) + jnp.where(
            events.reads, dot_t(grad_num, start_state), 0.0
        )
        out[1, h] = (slope(qf) * grad_phi_q + dq).astype(bf16)

    def start_stream(h):
        q = qs[h, :L, :]
        k = ks[h, p.tail_fill : B + L, :]
        v = vs[h, p.tail_fill : B + L, :]
        score = dot_t(q, k)
        yield
        phi_q = feature(q.astype(f32)).astype(bf16)
        a = dot_t(phi_q, feature(k[C:].astype(f32)).astype(bf16))
        if not p.far:
            near_out[h * D : (h + 1) * D, :] = halo_state(events_0, k[:C], v[:C], -C)
        yield
        low = events_0.low(win_ref[core * p.all + h])
        score = masked(events_0, score, low, -C)
        peak = jnp.max(score, axis=1, keepdims=True) * c2
        e = jnp.exp2(score * c2 - peak)
        peak_out[h] = wide_column(peak)
        total_out[h] = wide_column(jnp.sum(e, axis=1, keepdims=True))
        yield
        acc_out[h] = dot(e.astype(bf16), v)
        num_out[h] = dot(similar(events_0, a), v[C:])

    drive([stream(h) for h in range(p.all)] + [start_stream(h) for h in range(p.all)])
    stats_out[...] = stat_values(p, stat)


def first_body(p, core_ref, win_ref, *refs):
    near, far, refs = refs[:5], refs[5 : 5 + p.far_refs], refs[5 + p.far_refs :]
    begun, refs = refs[:5], refs[5:]
    acc_in, num_in, peak_in, total_in, near_state = begun
    (second_state, second_stats), refs = refs[:2], refs[2:]
    if p.far:
        far_ref, refs = refs[0], refs[1:]
    out, gn_out, stats_out, lse_out, rowdot_out, state_out, message, ks, vs, qs, gs, stat = refs
    core = core_ref[0]
    L, B, D = p.length, p.before, p.width
    scale, c2 = scales(p)
    own_keys_at, own_queries_at = own_chip(p, core, near)
    near_at = near_chip(p, core, near)
    own_queries_at.bring((qs, gs), 0, 0)
    far_codes = bring_far_keys(p, core, far, (ks, vs))
    halo_codes = jnp.concatenate([far_codes, near_at.codes()], axis=0)
    events = Events(p, 0, own_keys_at.codes(), halo_codes)

    def stream(h):
        q = qs[h]
        gf = gs[h].astype(f32)
        here = slice(h * D, (h + 1) * D)
        score = dot_t(q, ks[h])
        if p.far:
            start_state = far_ref[here, :]
        else:
            start_state = near_state[here, :] + halo_state(events, ks[h], vs[h], -B)
            start_state = start_state.astype(bf16)
        state_out[here, :] = start_state
        yield
        phi_q = feature(q.astype(f32)).astype(bf16)
        from_start = dot(phi_q, start_state)
        low = events.low(win_ref[core * p.all + h])
        s_pos = lax.broadcasted_iota(jnp.int32, score.shape, 1) - B
        score = jnp.where(s_pos >= low, score, MASKED) * c2
        old = peak_in[h]
        peak = jnp.maximum(old[:, 0:1], jnp.max(score, axis=1, keepdims=True))
        e = jnp.exp2(score - peak)
        yield
        kept = jnp.exp2(old - peak)
        total = total_in[h] * kept + jnp.sum(e, axis=1, keepdims=True)
        window_out = (acc_in[h] * kept + dot(e.astype(bf16), vs[h])) / total
        numerator = num_in[h] + jnp.where(events.reads, from_start, 0.0)
        linear_out, grad_num = normalized(numerator, gf)
        gn_out[h] = grad_num
        yield
        rowdot = jnp.sum(gf * window_out, axis=1, keepdims=True)
        out[h] = (linear_out + window_out).astype(bf16)
        opening = jnp.where(events.opening, phi_q, jnp.zeros_like(phi_q))
        message[here, :] = (second_state[here, :] + t_dot(opening, grad_num)).astype(bf16)
        lse = (peak + jnp.log2(total))[:, 0:1]
        lse_out[h] = wide_column(lse)
        rowdot_out[h] = wide_column(rowdot)
        yield
        put_stats(p, stat, h, lse, rowdot)

    drive(stream(h) for h in range(p.all))
    values = stat_values(p, stat)
    stats_out[...] = values
    for tile, values in enumerate((values, second_stats[...])):
        for n in range(3):
            piece = values.astype(bf16)
            at = p.state_rows + (3 * tile + n) * p.stat_rows
            message[at : at + p.stat_rows, :] = piece
            values = values - piece.astype(f32)


def grad_body(p, core_ref, win_ref, *refs):
    near, far, refs = refs[:5], refs[5 : 5 + p.far_refs], refs[5 + p.far_refs :]
    (first_out, gn, lse_in, rowdot_in, state_in, second), refs = refs[:6], refs[6:]
    keep, send, ks, vs, qs, gs, out = refs
    core = core_ref[0]
    L, B, D = p.length, p.before, p.width
    scale, c2 = scales(p)
    own_keys_at, own_queries_at = own_chip(p, core, near)
    near_at = near_chip(p, core, near)
    own_keys_at.bring((ks, vs), B, 0)
    own_queries_at.bring((qs, gs), 0, 0)
    near_at.bring((ks, vs), p.tail_fill)
    far_codes = bring_far_keys(p, core, far, (ks, vs))
    halo_codes = jnp.concatenate([far_codes, near_at.codes()], axis=0)
    events = Events(p, 0, own_keys_at.codes(), halo_codes)

    def stream(h):
        q = qs[h]
        score = dot_t(q, ks[h])
        grad_prob = dot_t(gs[h], vs[h])
        yield
        grad_num = gn[h]
        b = dot_t(grad_num, vs[h, B:, :])
        from_start = dot_t(grad_num, state_in[h * D : (h + 1) * D, :])
        yield
        low = events.low(win_ref[core * p.all + h])
        score = masked(events, score, low, -B)
        prob = jnp.exp2(score * c2 - lse_in[h][:, 0:1])
        ds = (prob * (grad_prob - rowdot_in[h][:, 0:1])).astype(bf16)
        yield
        dq = dot(ds, ks[h]) * scale
        phi_k = feature(ks[h, B:, :].astype(f32)).astype(bf16)
        grad_phi_q = dot(similar(events, b), phi_k) + jnp.where(events.reads, from_start, 0.0)
        yield
        out[0, h] = first_out[h]
        out[1, h] = (slope(q.astype(f32)) * grad_phi_q + dq).astype(bf16)

    drive(stream(h) for h in range(p.all))
    divide(core, (out, second), keep, send)


def query_side(p, core, windows, near, far, far_state, near_queries, far_queries):
    vmem = pl.BlockSpec(memory_space=pltpu.VMEM)
    smem = pl.BlockSpec(memory_space=pltpu.SMEM)

    def kernel(body, micros, args, outs, scratch):
        return pl.pallas_call(
            functools.partial(body, p),
            out_shape=[jax.ShapeDtypeStruct(shape, kind) for shape, kind in outs],
            in_specs=[smem, smem] + [vmem] * len(args),
            out_specs=[vmem] * len(outs),
            scratch_shapes=[pltpu.VMEM(shape, kind) for shape, kind in scratch],
            **params(micros),
            name=body.__name__,
        )(core, windows, *args)

    tile = (p.all, p.length, p.width)
    both = (2, *tile)
    stats = ((p.stat_rows, p.width), f32)
    state = (p.state_rows, p.width)
    rows = [(tile, bf16)] * 2
    far_state = [far_state] if p.far else []

    def keys(n):
        return [((p.all, n, p.width), bf16)] * 2

    second, grad_1, stats_1, state_1, *begun = kernel(
        second_body,
        8.0,
        [*near, *(() if p.merged else far), *far_state],
        [(both, bf16), (tile, bf16), stats, (state, f32)]
        + [(tile, f32)] * 2
        + [((p.all, p.length, LANES), f32)] * 2
        + [(state, f32)],
        keys(p.before + p.chip) + keys(p.chip) + [stats],
    )
    state_1, *_ = lax.optimization_barrier((state_1, *near_queries))
    first, grad_0, stats_0, lse, rowdot, start_state, message = kernel(
        first_body,
        2.0,
        [*near, *far, *begun, state_1, stats_1, *far_state],
        [(tile, bf16)] * 2
        + [stats]
        + [((p.all, p.length, LANES), f32)] * 2
        + [(state, bf16), ((p.state_rows + 6 * p.stat_rows, p.width), bf16)],
        keys(p.tail_fill) + rows + [stats],
    )

    def finish():
        return kernel(
            grad_body,
            3.5,
            [*near, *far, first, grad_0, lse, rowdot, start_state, second],
            [(both, bf16)] * 2,
            keys(p.before + p.length) + rows + [(both, bf16)],
        )

    return grad_1, stats_1, grad_0, stats_0, message, finish


def stats_of(p, values, head):
    result = []
    for which in range(2):
        base = (which * p.all + head) * p.code_rows
        result.append(flat(values[base : base + p.code_rows]))
    return result


def unpack_stats(p, message, tile):
    total = jnp.zeros((p.stat_rows, LANES), f32)
    for n in reversed(range(3)):
        at = p.state_rows + (3 * tile + n) * p.stat_rows
        total = total + message[at : at + p.stat_rows, :].astype(f32)
    return total


def own_body(p, core_ref, win_ref, *refs):
    near, grads, stats_in, refs = refs[:3], refs[3:5], refs[5:7], refs[7:]
    dk_o, dv_o, ks, vs, qs, gs = refs
    core = core_ref[0]
    L, C, D = p.length, p.chip, p.width
    scale = 1.0 / math.sqrt(D)
    c2 = scale * math.log2(math.e)
    own_keys_at, own_queries_at = own_chip(p, core, near)
    own_keys_at.bring((ks, vs), 0)
    own_queries_at.bring((qs, gs), 0)
    own_codes = own_keys_at.codes()
    code = column_of(own_codes)
    hi_all = jnp.zeros((C, 1), f32)
    for n in range(1, SESSIONS + 1):
        hi_all = jnp.where(code == n, count(own_codes <= n) - 1.0, hi_all)
    hi_all = hi_all.astype(jnp.int32)
    stats = [ref[...] for ref in stats_in]

    def stream(h, tile, r):
        window = win_ref[core * p.all + h]
        lse, rowdot = stats_of(p, stats[r], h)
        rows = slice(tile * L, (tile + 1) * L)
        k, v = ks[h, rows, :], vs[h, rows, :]
        after = slice(r * L, (r + 1) * L)
        q, g = qs[h, after, :], gs[h, after, :]
        score = dot_t(k, q)
        grad_prob = dot_t(v, g)
        yield
        phi_q = feature(q.astype(f32)).astype(bf16)
        kf = k.astype(f32)
        grad_num = grads[r][h]
        a = dot_t(feature(kf).astype(bf16), phi_q)
        b = dot_t(v, grad_num)
        yield
        hi = hi_all[rows]
        s_pos = lax.broadcasted_iota(jnp.int32, (L, 1), 0) + tile * L
        t_pos = lax.broadcasted_iota(jnp.int32, (L, L), 1) + r * L
        alike = t_pos <= hi
        if tile == r:
            alike = jnp.logical_and(alike, t_pos >= s_pos)
        allowed = jnp.logical_and(alike, t_pos < s_pos + window)
        prob = jnp.exp2(jnp.where(allowed, score * c2 - lse, MASKED))
        ds = (prob * (grad_prob - rowdot)).astype(bf16)
        yield
        dk = dot(ds, q) * scale
        dv = dot(prob.astype(bf16), g)
        a = jnp.where(alike, a, 0.0).astype(bf16)
        b = jnp.where(alike, b, 0.0).astype(bf16)
        yield
        dk = dk + slope(kf) * dot(b, phi_q)
        dv = dv + dot(a, grad_num)
        if r == 0:
            dk += dk_o[h, rows, :]
            dv += dv_o[h, rows, :]
        dk_o[h, rows, :] = dk
        dv_o[h, rows, :] = dv

    pairs = ((0, 1), (1, 1), (0, 0))
    drive(stream(h, tile, r) for tile, r in pairs for h in range(p.all))


def own_keys(p, core, windows, near, grads, stats):
    vmem = pl.BlockSpec(memory_space=pltpu.VMEM)
    smem = pl.BlockSpec(memory_space=pltpu.SMEM)
    full = jax.ShapeDtypeStruct((p.all, p.chip, p.width), f32)
    args = [*near[:3], *grads, *stats]
    keys = pltpu.VMEM((p.all, p.chip, p.width), bf16)
    return pl.pallas_call(
        functools.partial(own_body, p),
        out_shape=[full, full],
        in_specs=[smem, smem] + [vmem] * len(args),
        out_specs=[vmem] * 2,
        scratch_shapes=[keys] * 4,
        **params(5.0),
        name="own_keys",
    )(core, windows, *args)


def later_body(p, core_ref, win_ref, *refs):
    near, refs = refs[:5], refs[5:]
    far, refs = refs[: p.far_refs], refs[p.far_refs :]
    (message_1, message_2, dk_i, dv_i), refs = refs[:4], refs[4:]
    if p.far:
        far_ref, refs = refs[0], refs[1:]
    keep, send, ks, vs, qs, gs, first, second = refs
    core = core_ref[0]
    L, C, D = p.length, p.chip, p.width
    N = p.tail_fill
    scale = 1.0 / math.sqrt(D)
    c2 = scale * math.log2(math.e)
    own_keys_at, _ = own_chip(p, core, near)
    near_at = near_chip(p, core, near)
    own_keys_at.bring((ks, vs), 0)
    near_at.bring((qs, gs), 0)
    own_codes = own_keys_at.codes()
    near_codes = near_at.codes()
    if p.merged:
        far_codes = code_block(p, far[0])
        bring_tail(p, far[0], (qs, gs), C)
        if p.tail < p.tail_fill:
            gap = p.tail_fill - p.tail
            qs[:, C + p.tail :, :] = jnp.zeros((p.all, gap, D), bf16)
            gs[:, C + p.tail :, :] = jnp.zeros((p.all, gap, D), bf16)
    else:
        far_at = Chip(p, core, *far)
        far_at.bring((qs, gs), C)
        far_codes = far_at.codes()
    after_codes = jnp.concatenate([near_codes, far_codes], axis=0)
    code = column_of(own_codes)
    final = own_codes[2 * p.code_rows - 1 :, LANES - 1 :]
    hi_last = C - 1 + count(after_codes == final)
    hi = jnp.where(code == final, hi_last, -1.0).astype(jnp.int32)
    first_next = near_codes[0:1, 0:1]
    goes_on = jnp.logical_and(first_next > 0, first_next == far_codes[0:1, 0:1])
    tiles = [unpack_stats(p, message_1, 0), unpack_stats(p, message_1, 1)]
    tiles += [unpack_stats(p, message_2, n) for n in range(N // L)]

    def stream(h, r):
        far_here = r == 1 or not p.merged
        wide = C + N if far_here else C
        rows = slice(r * L, (r + 1) * L)
        uses = code[rows] == first_next
        window = win_ref[core * p.all + h]
        lse, rowdot = (
            jnp.concatenate(x, axis=1) for x in zip(*(stats_of(p, tile, h) for tile in tiles[: wide // L]))
        )
        k, v = ks[h, rows, :], vs[h, rows, :]
        q, g = qs[h, 0:wide, :], gs[h, 0:wide, :]
        score = dot_t(k, q)
        grad_prob = dot_t(v, g)
        yield
        here = slice(h * D, (h + 1) * D)
        if p.far:
            later_state = far_ref[here, :]
        else:
            later_state = message_1[here, :]
            if far_here:
                later_state = (
                    later_state.astype(f32)
                    + jnp.where(goes_on, message_2[here, :].astype(f32), 0.0)
                ).astype(bf16)
        kf = k.astype(f32)
        phi_k = feature(kf).astype(bf16)
        dk_lin = dot_t(v, later_state)
        dv_lin = dot(phi_k, later_state)
        yield
        s_pos = lax.broadcasted_iota(jnp.int32, (L, 1), 0) + r * L
        t_pos = lax.broadcasted_iota(jnp.int32, (L, wide), 1) + C
        allowed = t_pos <= jnp.minimum(hi[rows], s_pos + window - 1)
        prob = jnp.exp2(jnp.where(allowed, score * c2 - lse, MASKED))
        ds = (prob * (grad_prob - rowdot)).astype(bf16)
        yield
        dk = dot(ds, q) * scale
        dv = dot(prob.astype(bf16), g)
        yield
        out = (first, second)[r]
        dk = dk_i[h, rows, :] + dk + slope(kf) * jnp.where(uses, dk_lin, 0.0)
        dv = dv_i[h, rows, :] + dv + jnp.where(uses, dv_lin, 0.0)
        out[0, h] = dk.astype(bf16)
        out[1, h] = dv.astype(bf16)

    drive(stream(h, r) for h in range(p.all) for r in range(2))
    divide(core, (first, second), keep, send)


def later_keys(p, core, windows, near, far, messages, sums, far_state):
    vmem = pl.BlockSpec(memory_space=pltpu.VMEM)
    smem = pl.BlockSpec(memory_space=pltpu.SMEM)
    args = [*near, *far, *messages, *sums] + ([far_state] if p.far else [])
    both = jax.ShapeDtypeStruct((2, p.all, p.length, p.width), bf16)
    keys = pltpu.VMEM((p.all, p.chip, p.width), bf16)
    tall = pltpu.VMEM((p.all, p.chip + p.tail_fill, p.width), bf16)
    return pl.pallas_call(
        functools.partial(later_body, p),
        out_shape=[both, both],
        in_specs=[smem, smem] + [vmem] * len(args),
        out_specs=[vmem, vmem],
        scratch_shapes=[keys, keys, tall, tall] + [pltpu.VMEM(both.shape, bf16)] * 2,
        **params(5.5),
        name="later_keys",
    )(core, windows, *args)


def unpack_body(p, core_ref, mine, theirs, out_a, out_b, scratch):
    core = core_ref[0]
    for n in range(2):
        for h in range(p.all):
            scratch[n, core * p.all + h] = mine[n, h].astype(f32)
            scratch[n, (1 - core) * p.all + h] = theirs[n, h].astype(f32)
    for n, out in ((0, out_a), (1, out_b)):
        out[...] = jnp.swapaxes(scratch[n], 0, 1).astype(bf16)


def unpack(p, core, mine, theirs):
    vmem = pl.BlockSpec(memory_space=pltpu.VMEM)
    out = jax.ShapeDtypeStruct((p.length, p.heads, p.width), bf16)
    return pl.pallas_call(
        functools.partial(unpack_body, p),
        out_shape=[out, out],
        in_specs=[pl.BlockSpec(memory_space=pltpu.SMEM)] + [vmem] * 2,
        out_specs=[vmem, vmem],
        scratch_shapes=[pltpu.VMEM((2, p.heads, p.length, p.width), f32)],
        **params(1.4),
        name="unpack",
    )(core, mine, theirs)


def folded(session, state, backward):
    sessions = lax.all_gather(session, "ctx")
    states = lax.all_gather(state, "ctx")
    count = lax.axis_size("ctx")
    here = lax.axis_index("ctx")

    def one(hop, carry):
        held, total = carry
        source = count - 1 - hop if backward else hop
        new = lax.dynamic_index_in_dim(sessions, source, 0, False)
        first, last = new[0], new[1]
        part = lax.dynamic_index_in_dim(states, source, 0, False).astype(f32)
        entering, leaving = (last, first) if backward else (first, last)
        whole = jnp.logical_and(entering == held, entering == leaving)
        return leaving, part + jnp.where(whole, total, 0.0)

    steps = count - 1 - here if backward else here
    start = (jnp.zeros((), jnp.int32) - 1, jnp.zeros(state.shape, f32))
    return lax.fori_loop(0, steps, one, start)[1].astype(bf16)


def shards(p, queries, key_vectors, value_vectors, targets, token_weights, sessions, window_size):
    L = p.length
    chips = lax.axis_size("ctx")
    core_id = lax.axis_index("pair").astype(jnp.int32)
    core = core_id.reshape(1)
    def move(x, target):
        pairs = []
        for c in range(chips):
            for i in range(2):
                to, j = target(c, i)
                if 0 <= to < chips:
                    pairs.append((2 * c + i, 2 * to + j))
        return lax.ppermute(x, AXES, pairs)

    packed = pack(
        p,
        core,
        queries,
        key_vectors,
        value_vectors,
        targets,
        token_weights.reshape(-1, LANES),
        sessions.reshape(-1, LANES),
    )
    for_pair, payloads = packed[0], packed[1:]

    def exchange(same, cross, by):
        return (
            move(same, lambda c, i: (c + by, i)),
            move(cross, lambda c, i: (c + by, 1 - i)),
        )

    pair = move(for_pair, lambda c, i: (c, 1 - i))
    kv_same, kv_cross, qg_same, qg_cross = payloads
    near_keys = exchange(kv_same, kv_cross, 1)
    near_queries = exchange(qg_same, qg_cross, -1)
    if p.merged:
        last_keys, first_queries = make_tails(p, core, pair, kv_same, qg_same)
        last_keys, key_part = lax.optimization_barrier((last_keys, near_keys[0]))
        near_keys = (key_part, near_keys[1])
        first_queries, query_part = lax.optimization_barrier((first_queries, near_queries[0]))
        near_queries = (query_part, near_queries[1])
        far_keys = (move(last_keys, lambda c, i: (c + 2, i)),)
        far_queries = (move(first_queries, lambda c, i: (c - 2, i)),)
    else:
        far_keys = exchange(kv_same, kv_cross, 2)
        far_queries = exchange(qg_same, qg_cross, -2)
    own = (pair, kv_same, qg_same)
    near = (*own, *near_keys)

    far_before = far_after = None
    if p.far:
        both = lax.all_gather(sessions, "pair")
        chip_ends = jnp.stack([both[0, 0], both[1, -1]])

        total = jnp.zeros((p.all, p.width, p.width), f32)
        keys_here = kv_same[: p.rows - EXTRA]
        keys_here = keys_here.reshape(2, p.all, L, p.width)
        keys_pair = pair[: p.pair_rows - EXTRA].reshape(4, p.all, L, p.width)[:2]
        for part, owner in ((keys_here, core_id), (keys_pair, 1 - core_id)):
            rows = lax.dynamic_index_in_dim(both, owner, 0, False)
            phi = feature(part[0].astype(f32))
            phi = jnp.where((rows == chip_ends[1])[None, :, None], phi, 0.0).astype(bf16)
            total = total + jnp.einsum(
                "hsk,hsd->hkd", phi, part[1], preferred_element_type=f32
            )
        far_before = folded(chip_ends, total.astype(bf16), False).reshape(-1, p.width)

    grad_1, stats_1, grad_0, stats_0, message, finish = query_side(
        p, core, window_size, near, far_keys, far_before, near_queries, far_queries
    )
    message, grad_1 = lax.optimization_barrier((message, grad_1))
    messages = (
        move(message, lambda c, i: (c - 1, i)),
        move(message, lambda c, i: (c - 2, i)),
    )
    if p.far:
        state = message[: p.state_rows].reshape(p.all, p.width, p.width)
        far_after = folded(chip_ends, state, True).reshape(-1, p.width)
    keep_q, send_q = finish()
    sums = own_keys(p, core, window_size, near, (grad_0, grad_1), (stats_0, stats_1))
    keep_k, send_k = later_keys(
        p, core, window_size, (*own, *near_queries), far_queries, messages, sums, far_after
    )
    attended, grad_queries = unpack(p, core, keep_q, move(send_q, lambda c, i: (c, 1 - i)))
    grad_keys, grad_values = unpack(p, core, keep_k, move(send_k, lambda c, i: (c, 1 - i)))
    return (attended, grad_queries, grad_keys, grad_values)


def solution(mesh):
    rows = P(("groups", "ctx", "pair"), "head", None)
    events = P(("groups", "ctx", "pair"))

    def run(queries, key_vectors, value_vectors, targets, token_weights, sessions, window_size):
        total = queries.shape[0] // mesh.shape["groups"]
        length = total // (mesh.shape["ctx"] * mesh.shape["pair"])
        heads = queries.shape[1] // mesh.shape["head"]
        p = Plan(length, heads, queries.shape[2], total)
        return jax.shard_map(
            functools.partial(shards, p),
            mesh=mesh,
            in_specs=(rows, rows, rows, rows, events, events, P("head")),
            out_specs=(rows, rows, rows, rows),
            check_vma=False,
        )(queries, key_vectors, value_vectors, targets, token_weights, sessions, window_size)

    return run
```
